256 devices in a mesh: row: 8 (over y, x_hi), col: 32 (over z, x_lo, core).
Axes of the slice: x: 4 (x_hi: 2, x_lo: 2; x = x_hi * 2 + x_lo), y: 4, z: 8, core: 2. Of those that a mesh axis runs over, the one named last changes fastest.
Arguments:
- gradient: bfloat16 [8192, 8192], P('row', 'col'), may hold values from -0.6 to 0.6
- left_old: float32 [8192, 8192], P('row', 'col'), may hold values from -6 to 6
- right_old: float32 [8192, 8192], P('row', 'col'), may hold values from -6 to 6
Outputs:
- left_factor: float32 [8192, 8192], P('row', 'col')
- right_factor: float32 [8192, 8192], P('row', 'col')
The draws below stay inside these ranges and needn't reach their ends.
All inputs are finite; a program needn't handle non-finite values.
Results may differ from the reference program's by a relative error of at most 0.0003.
Values may be sent and summed in bfloat16 or wider, within the bound.
A program may use at most 128 MiB of HBM per device.

```python
import jax
import jax.numpy as jnp
from jax import lax

ROWS = 8192
COLS = 8192


def draw_gradient(key, part):
    key = jax.random.fold_in(key, 11)
    first = jax.random.fold_in(key, 0)
    values = 0.1 * jax.random.normal(first, (ROWS, COLS), jnp.float32)
    return jnp.clip(values, -0.6, 0.6).astype(jnp.bfloat16)


def block_levels(stream_key, extent, shards, low, high):
    def one(axis_at, blocks):
        steps = jax.random.uniform(jax.random.fold_in(jax.random.fold_in(stream_key, 6), axis_at), (blocks,), jnp.float32, low / len(shards), high / len(shards))
        return jnp.repeat(jnp.exp(steps), extent[axis_at] // blocks).reshape((-1,) + (1,) * (len(extent) - axis_at - 1))

    level = one(*shards[0])
    for cut in shards[1:]:
        level = level * one(*cut)
    return level


def normal_values(stream_key, dims, spread, bound, cuts=(), held_as=jnp.bfloat16):
    array = jax.random.normal(stream_key, dims, jnp.float32) * spread
    if len(cuts) > 0:
        array = block_levels(stream_key, dims, cuts, -0.22, 0.18) * array
    return jnp.clip(array, min=-bound, max=bound).astype(held_as)


def setup_inputs(seed: int = 0) -> dict:
    key_list = jax.random.split(jax.random.key(seed), 4)
    return {
        "gradient": draw_gradient(jax.random.fold_in(key_list[3], 71), 0),
        "left_old": normal_values(key_list[1], (ROWS, ROWS), 0.5, 6.0, ((0, 8), (1, 32)), jnp.float32),
        "right_old": normal_values(key_list[2], (COLS, COLS), 0.5, 6.0, ((0, 8), (1, 32)), jnp.float32),
    }


def reference(gradient, left_old, right_old):
    gram_left = lax.dot_general(gradient, gradient, (((1,), (1,)), ((), ())), preferred_element_type=jnp.float32)
    left_factor = 0.95 * left_old + 0.05 * gram_left
    gram_right = lax.dot_general(gradient, gradient, (((0,), (0,)), ((), ())), preferred_element_type=jnp.float32)
    right_factor = 0.95 * right_old + 0.05 * gram_right
    return left_factor, right_factor
```

```python
import jax
import jax.numpy as jnp
from jax import lax
from jax.experimental import pallas as pl
from jax.experimental.pallas import tpu as pltpu
from jax.sharding import PartitionSpec as P

MESH = pl.DeviceIdType.MESH
BF16, F32 = jnp.bfloat16, jnp.float32
ROW = 1024
SUB = 256
RING = 8
DEPTH = RING * SUB
CHUNK = 16
STEPS = 512 // CHUNK
HALF = STEPS // 2
LAG = 3
ADD, END = 3, 8


def at(start, size):
    return pl.ds(pl.multiple_of(start, size), size)


def kernel(g_ref, lo_ref, ro_ref, l_ref, r_ref,
           grad, turned, own, rec, prod_l, prod_r, core_l, core_r, chip_l, chip_r, last_l, last_r, total, old, out,
           load_sem, swap_send, swap_recv, mix_send, mix_recv, ag_send, ag_recv, bc_send, bc_recv, own_sem,
           core_send, core_recv, chip_send, chip_recv, out_sem):
    a, j = lax.axis_index("row"), lax.axis_index("col")
    y, h = a // 2, a % 2
    z, l, c = j // 4, (j // 2) % 2, j % 2
    p = jnp.where(h == 0, y, 7 - y)
    mine = l * 2 + c

    def plane(step):
        q = (p + step + RING) % RING
        h2 = q // 4
        y2 = jnp.where(h2 == 0, q, 7 - q)
        return (y2 * 2 + h2, z * 4 + ((l + h + h2) % 2) * 2 + c)

    def line(step):
        return (a, ((z + step + RING) % RING) * 4 + mine)

    def inside(dl, dc):
        return (a, z * 4 + ((l + dl) % 2) * 2 + (c + dc) % 2)

    sides = (line(1), line(-1), plane(1), plane(-1))
    mate, twin = inside(0, 1), inside(1, 0)

    grad_in = pltpu.make_async_copy(g_ref, grad, load_sem.at[0])
    grad_in.start()
    old_in = [pltpu.make_async_copy(ref, old.at[q], load_sem.at[1 + q]) for q, ref in enumerate((lo_ref, ro_ref))]
    for copy in old_in:
        copy.start()

    barrier = pltpu.get_barrier_semaphore()
    for device in sides + (mate, twin, inside(1, 1)):
        pl.semaphore_signal(barrier, inc=1, device_id=device, device_id_type=MESH)
    pl.semaphore_wait(barrier, 7)

    def swap(u):
        rows = pl.ds(u * SUB, SUB)
        return pltpu.make_async_remote_copy(
            src_ref=g_ref.at[rows], dst_ref=own.at[0, rows, at(z * SUB, SUB)],
            send_sem=swap_send.at[u], recv_sem=swap_recv.at[u], device_id=twin, device_id_type=MESH)

    for u in range(4):
        @pl.when(h == 0)
        def _():
            rows = pl.ds(u * SUB, SUB)
            pltpu.make_async_copy(g_ref.at[rows], own.at[0, rows, at(z * SUB, SUB)], swap_recv.at[u]).start()

        @pl.when(h == 1)
        def _():
            swap(u).start()

    grad_in.wait()
    for u in range(4):
        turned[:, u * SUB:(u + 1) * SUB] = grad[u * SUB:(u + 1) * SUB, :].T

    def mix(dl, dc):
        part = ((l + dl + h) % 2) * 2 + (c + dc) % 2
        src = turned.at[:, at(part * SUB, SUB)]
        dst = own.at[1, at(mine * SUB, SUB), at(a * SUB, SUB)]
        if dl == dc == 0:
            return pltpu.make_async_copy(src, dst, mix_recv.at[mine])
        return pltpu.make_async_remote_copy(
            src_ref=src, dst_ref=dst, send_sem=mix_send.at[dl * 2 + dc], recv_sem=mix_recv.at[mine],
            device_id=inside(dl, dc), device_id_type=MESH)

    for dl, dc in ((1, 0), (1, 1), (0, 1), (0, 0)):
        mix(dl, dc).start()

    def gather(r, q):
        prob, sign = r // 2, 1 - 2 * (r % 2)
        step = q // 4
        u = (q + 2 * (r % 2)) % 4
        if prob == 0:
            k = (z - sign * step + RING) % RING
        else:
            k = (p - sign * step + RING) % RING
            k = jnp.where(k < 4, 2 * k, 15 - 2 * k)
        part = own.at[prob, at(u * SUB, SUB), at(k * SUB, SUB)]
        return pltpu.make_async_remote_copy(
            src_ref=part, dst_ref=part, send_sem=ag_send.at[r], recv_sem=ag_recv.at[r, q],
            device_id=sides[r], device_id_type=MESH)

    for u in range(4):
        rows = pl.ds(u * SUB, SUB)
        here = own.at[0, rows, at(z * SUB, SUB)]
        pltpu.make_async_copy(here, here, swap_recv.at[u]).wait()
        gather(0, u).start()
        gather(1, (u + 2) % 4).start()
    for u in range(4):
        rows = pl.ds(u * SUB, SUB)
        here = own.at[1, rows, at(a * SUB, SUB)]
        pltpu.make_async_copy(here, here, mix_recv.at[u]).wait()
        gather(2, u).start()
        gather(3, (u + 2) % 4).start()

    @pl.loop(4, 14)
    def _(q):
        for r in range(4):
            gather(r, q - 4).wait_recv()
            gather(r, q).start()

    @pl.loop(10, 14)
    def _(q):
        for r in range(4):
            gather(r, q).wait_recv()

    for copy in old_in:
        copy.wait()

    first = jnp.where(z % 2 == 0, z // 2, 7 - z // 2)
    away = ((p - first + RING) % RING, (first - p + RING) % RING, (z - a + RING) % RING, (a - z + RING) % RING)
    onward = (sides[2], sides[3], sides[0], sides[1])

    def own_copy(prob, g, s):
        src = s * SUB + g * 64 if prob == 0 else g * SUB + s * 64
        return pltpu.make_async_copy(own.at[prob, at(src, 64)], rec.at[prob, at(g * SUB + s * 64, 64)], own_sem.at[prob])

    for prob in range(2):
        @pl.when(away[prob * 2] == 0)
        def _():
            @pl.loop(0, 16)
            def _(n):
                own_copy(prob, n // 4, n % 4).start()

    prods, cores, chips, lasts = (prod_l, prod_r), (core_l, core_r), (chip_l, chip_r), (last_l, last_r)

    def to_mate(prob, g):
        return pltpu.make_async_remote_copy(
            src_ref=prods[prob].at[g, 1 - c], dst_ref=cores[prob].at[g],
            send_sem=core_send.at[prob, g], recv_sem=core_recv.at[prob, g], device_id=mate, device_id_type=MESH)

    def to_twin(prob, g):
        return pltpu.make_async_remote_copy(
            src_ref=chips[prob].at[g], dst_ref=lasts[prob].at[g],
            send_sem=chip_send.at[prob, g], recv_sem=chip_recv.at[prob, g], device_id=twin, device_id_type=MESH)

    def out_copy(prob, n):
        if prob == 0:
            cols = pl.ds(n * 128, 128)
            return pltpu.make_async_copy(out.at[0, :, cols], l_ref.at[:, cols], out_sem.at[0, n])
        rows = at(n * SUB, SUB)
        return pltpu.make_async_copy(out.at[1, rows], r_ref.at[rows], out_sem.at[1, n])

    def multiply(prob, g):
        @pl.loop(0, 4)
        def _(n):
            tile = lax.dot_general(
                rec[prob, at(g * SUB, SUB), :], own[prob, at(n * SUB, SUB), :],
                (((1,), (1,)), ((), ())), preferred_element_type=F32)
            if prob == 0:
                for s in range(4):
                    prod_l[g, s % 2, s // 2, :, at(n * SUB, SUB)] = tile[s * 64:(s + 1) * 64, :]
            else:
                prod_r[g, n % 2, n // 2] = tile
        to_mate(prob, g).start()

    def add(prob, g):
        to_mate(prob, g).wait_recv()
        chips[prob][g] = prods[prob][g, c, 1 - l] + cores[prob][g, 1 - l]
        to_twin(prob, g).start()

    def finish(prob, st, gl):
        g = st * 2 + gl
        to_twin(prob, g).wait_recv()
        value = prods[prob][g, c, l] + cores[prob][g, l] + lasts[prob][g]
        if prob == 1:
            rows = at(g * SUB, SUB)
            out[1, rows, :] = 0.95 * old[1, rows, :] + 0.05 * value
            out_copy(1, g).start()
        else:
            total[at(g * 64, 64), :] = value

            @pl.when(gl == 1)
            def _():
                cols = slice(st * 128, (st + 1) * 128)
                for n in range(4):
                    rows = slice(n * 256, (n + 1) * 256)
                    out[0, rows, cols] = 0.95 * old[0, rows, cols] + 0.05 * total[cols, rows].T
                out_copy(0, st).start()

    def pass_on(i, n, src):
        dst = rec.at[i // 2, at((i % 2) * 512 + n * CHUNK, CHUNK)]
        return pltpu.make_async_remote_copy(
            src_ref=dst if src is None else src, dst_ref=dst, send_sem=bc_send.at[i], recv_sem=bc_recv.at[i, n],
            device_id=onward[i], device_id_type=MESH)

    @pl.loop(0, STEPS + END + LAG * (RING - 1))
    def _(t):
        for i in range(4):
            prob, st = i // 2, i % 2
            n = t - LAG * away[i]

            @pl.when((n >= 0) & (n < STEPS))
            def _():
                @pl.when(away[i] == 0)
                def _():
                    if prob == 0:
                        g, s, m = st * 2 + n // HALF, (n % HALF) // (HALF // 4), n % (HALF // 4)
                        row = s * SUB + g * 64 + m * CHUNK
                    else:
                        row = st * 512 + n * CHUNK
                    pass_on(i, n, own.at[prob, at(row, CHUNK)]).start()

                @pl.when(away[i] > 0)
                def _():
                    pass_on(i, n, None).wait_recv()

                @pl.when((away[i] > 0) & (away[i] < RING - 1))
                def _():
                    pass_on(i, n, None).start()

        for i in range(4):
            prob, st = i // 2, i % 2
            n = t - LAG * away[i]

            @pl.when((n == HALF - 1) | (n == STEPS - 1))
            def _():
                if st == 0:
                    @pl.when((away[i] == 0) & (n == HALF - 1))
                    def _():
                        pltpu.make_async_copy(own.at[prob], rec.at[prob], own_sem.at[prob]).wait()
                multiply(prob, st * 2 + n // HALF)

            @pl.when((n == HALF - 1 + ADD) | (n == STEPS - 1 + ADD))
            def _():
                add(prob, st * 2 + (n - ADD) // HALF)

            @pl.when((n == HALF - 1 + END) | (n == STEPS - 1 + END))
            def _():
                finish(prob, st, (n - END) // HALF)

    for r in range(4):
        sent = own.at[r // 2, pl.ds(0, 14 * SUB * SUB // DEPTH)]
        pltpu.make_async_copy(sent, sent, ag_send.at[r]).wait()
    for i in range(4):
        @pl.when(away[i] < RING - 1)
        def _():
            sent = rec.at[i // 2, pl.ds(0, 512)]
            pltpu.make_async_copy(sent, sent, bc_send.at[i]).wait()

    @pl.when(h == 1)
    def _():
        for u in range(4):
            swap(u).wait_send()
    for dl, dc in ((1, 0), (1, 1), (0, 1)):
        mix(dl, dc).wait_send()
    for prob in range(2):
        for g in range(4):
            to_mate(prob, g).wait_send()
            to_twin(prob, g).wait_send()
    for prob in range(2):
        for n in range(2 + 2 * prob):
            out_copy(prob, n).wait()


def on_device(gradient, left_old, right_old):
    factor = jax.ShapeDtypeStruct((ROW, SUB), F32)
    anywhere = pl.BlockSpec(memory_space=pl.ANY)
    dma = pltpu.SemaphoreType.DMA
    return pl.pallas_call(
        kernel,
        out_shape=(factor, factor),
        in_specs=[anywhere] * 3,
        out_specs=(anywhere, anywhere),
        scratch_shapes=[
            pltpu.VMEM((ROW, SUB), BF16), pltpu.VMEM((SUB, ROW), BF16),
            pltpu.VMEM((2, ROW, DEPTH), BF16), pltpu.VMEM((2, ROW, DEPTH), BF16),
            pltpu.VMEM((4, 2, 2, 64, ROW), F32), pltpu.VMEM((4, 2, 2, SUB, SUB), F32),
            pltpu.VMEM((4, 2, 64, ROW), F32), pltpu.VMEM((4, 2, SUB, SUB), F32),
            pltpu.VMEM((4, 64, ROW), F32), pltpu.VMEM((4, SUB, SUB), F32),
            pltpu.VMEM((4, 64, ROW), F32), pltpu.VMEM((4, SUB, SUB), F32),
            pltpu.VMEM((SUB, ROW), F32), pltpu.VMEM((2, ROW, SUB), F32), pltpu.VMEM((2, ROW, SUB), F32),
            dma((3,)), dma((4,)), dma((4,)), dma((4,)), dma((4,)), dma((4,)), dma((4, 14)), dma((4,)), dma((4, STEPS)),
            dma((2,)), dma((2, 4)), dma((2, 4)), dma((2, 4)), dma((2, 4)), dma((2, 4)),
        ],
        compiler_params=pltpu.CompilerParams(collective_id=0, has_side_effects=True, vmem_limit_bytes=56 << 20),
        cost_estimate=pl.CostEstimate(flops=4 * ROW * SUB * 8192, bytes_accessed=5 << 20, transcendentals=0),
        name="gram_factors",
    )(gradient, left_old, right_old)


def solution(mesh):
    placed = (P("row", "col"), P("row", "col"), P("row", "col"))
    return jax.shard_map(
        on_device,
        mesh=mesh,
        in_specs=placed,
        out_specs=(P("row", "col"), P("row", "col")),
        check_vma=False,
    )
```

```python
import jax
import jax.numpy as jnp
from jax import lax
from jax.experimental import pallas as pl
from jax.experimental.pallas import tpu as pltpu
from jax.sharding import PartitionSpec as P

MESH = pl.DeviceIdType.MESH
BF16, F32 = jnp.bfloat16, jnp.float32
ROW = 1024
SUB = 256
RING = 8
DEPTH = RING * SUB
CHUNK = 16
COUNT = (22, 21, 21)
LAG = 3
ADD, END = 6, 12
READY = (5, 10, 15, 21)
LEVEL = ((0, 3, 1, 2, 2, 3, 3, 4), (0, 3, 3, 4, 2, 3, 1, 2), (0, 1, 3, 2, 4, 3, 3, 2))
ONWARD = (((0, 2, 4, 5), (3,), (2, 4)), ((7,), (0, 6, 4, 7, 5), (6,)), ((1, 3), (1,), (0, 3, 7, 5)))
FAR, HERE = 3, 4


def at(start, size):
    return pl.ds(pl.multiple_of(start, size), size)


def one_of(value, choices):
    found = value == choices[0]
    for choice in choices[1:]:
        found = found | (value == choice)
    return found


def lookup(index, values):
    result = jnp.int32(0)
    for place, value in enumerate(values):
        result = result + jnp.where(index == place, value, 0)
    return result


def kernel(g_ref, lo_ref, ro_ref, l_ref, r_ref,
           grad, turned, own, rec, prod_l, core_l, chip_l, last_l, total, prod_r, core_r, chip_r, last_r, sum_r, stage, old, out,
           load_sem, swap_send, swap_recv, mix_send, mix_recv, line_send, line_recv, x_send, x_recv, y_send, y_recv,
           slice_send, slice_recv, tree_send, tree_recv, own_sem,
           lcore_send, lcore_recv, lchip_send, lchip_recv, rcore_send, rcore_recv, rchip_send, rchip_recv,
           home_send, home_recv, out_sem):
    a, j = lax.axis_index("row"), lax.axis_index("col")
    y, h = a // 2, a % 2
    z, l, c = j // 4, (j // 2) % 2, j % 2
    mine = l * 2 + c

    def line(step):
        return (a, ((z + step + RING) % RING) * 4 + mine)

    def along_y(step):
        return (((y + step + 4) % 4) * 2 + h, j)

    def inside(dl, dc):
        return (a, z * 4 + ((l + dl) % 2) * 2 + (c + dc) % 2)

    def in_plane(row):
        return (row, z * 4 + ((l + h + row) % 2) * 2 + c)

    lines = (line(1), line(-1))
    mate, twin = inside(0, 1), inside(1, 0)
    across = (y * 2 + 1 - h, z * 4 + (1 - l) * 2 + c)
    plane = (along_y(1), along_y(-1), across)

    grad_in = pltpu.make_async_copy(g_ref, grad, load_sem.at[0])
    grad_in.start()
    old_in = [pltpu.make_async_copy(ref, old.at[q], load_sem.at[1 + q]) for q, ref in enumerate((lo_ref, ro_ref))]
    for copy in old_in:
        copy.start()

    def kept(u):
        rows = pl.ds(u * 512, 512)
        return pltpu.make_async_copy(
            g_ref.at[rows, at(h * 128, 128)], own.at[0, rows, at(z * SUB + h * 128, 128)], swap_recv.at[u])

    def swap(u):
        rows = pl.ds(u * 512, 512)
        return pltpu.make_async_remote_copy(
            src_ref=g_ref.at[rows, at((1 - h) * 128, 128)], dst_ref=own.at[0, rows, at(z * SUB + (1 - h) * 128, 128)],
            send_sem=swap_send.at[u], recv_sem=swap_recv.at[2 + u], device_id=twin, device_id_type=MESH)

    kept(0).start()
    kept(1).start()

    barrier = pltpu.get_barrier_semaphore()
    for device in lines + (mate, twin, inside(1, 1)):
        pl.semaphore_signal(barrier, inc=1, device_id=device, device_id_type=MESH)
    for step in range(1, RING):
        pl.semaphore_signal(barrier, inc=1, device_id=in_plane((a + step) % RING), device_id_type=MESH)
    pl.semaphore_wait(barrier, 12)

    swap(0).start()
    swap(1).start()

    def gather(r, q):
        step, u = q // 4, q % 4
        if r == 1:
            u = u + jnp.where(step == 3, 2, 0)
        k = (z - (1 - 2 * r) * step + RING) % RING
        side = jnp.where(u < 2, h, 1 - h)
        part = own.at[0, at((u % 2) * 512, 512), at(k * SUB + side * 128, 128)]
        return pltpu.make_async_remote_copy(
            src_ref=part, dst_ref=part, send_sem=line_send.at[r], recv_sem=line_recv.at[r, q],
            device_id=lines[r], device_id_type=MESH)

    for u in range(2):
        kept(u).wait()
        gather(0, u).start()
        gather(1, u).start()

    grad_in.wait()
    for u in range(4):
        turned[:, u * SUB:(u + 1) * SUB] = grad[u * SUB:(u + 1) * SUB, :].T

    def mix(dl, dc):
        part = ((l + dl + h) % 2) * 2 + (c + dc) % 2
        src = turned.at[:, at(part * SUB, SUB)]
        dst = own.at[1, at(mine * SUB, SUB), at(a * SUB, SUB)]
        if dl == dc == 0:
            return pltpu.make_async_copy(src, dst, mix_recv.at[mine])
        return pltpu.make_async_remote_copy(
            src_ref=src, dst_ref=dst, send_sem=mix_send.at[dl * 2 + dc], recv_sem=mix_recv.at[mine],
            device_id=inside(dl, dc), device_id_type=MESH)

    for dl, dc in ((1, 0), (1, 1), (0, 1), (0, 0)):
        mix(dl, dc).start()

    def in_y(r, n):
        late = n >= 8
        kind = jnp.where(late, (n - 8) // 2, n // 4)
        v = jnp.where(late, (n - 8) % 2 + 2 * r, n % 4)
        from_y = (y - jnp.where(late, 1 - 2 * r, 0) + 4) % 4
        k = from_y * 2 + (h + kind) % 2
        u = (v + 2 * ((l + kind) % 2)) % 4
        part = own.at[1, at(u * SUB, SUB), at(k * SUB, SUB)]
        return pltpu.make_async_remote_copy(
            src_ref=part, dst_ref=part, send_sem=y_send.at[r], recv_sem=y_recv.at[r, n],
            device_id=plane[r], device_id_type=MESH)

    def over_x(u):
        part = own.at[1, at(u * SUB, SUB), at(a * SUB, SUB)]
        return pltpu.make_async_remote_copy(
            src_ref=part, dst_ref=part, send_sem=x_send.at[0], recv_sem=x_recv.at[u], device_id=across, device_id_type=MESH)

    for u in range(2):
        swap(u).wait_recv()
        gather(0, 2 + u).start()
        gather(1, 2 + u).start()
    for v in range(4):
        u = (v + 2 * l) % 4
        here = own.at[1, at(u * SUB, SUB), at(a * SUB, SUB)]
        pltpu.make_async_copy(here, here, mix_recv.at[u]).wait()
        over_x(u).start()
        in_y(0, v).start()
        in_y(1, v).start()

    @pl.loop(4, 14)
    def _(q):
        gather(0, q - 4).wait_recv()
        gather(0, q).start()
        gather(1, q - jnp.where(q < 12, 4, 2)).wait_recv()
        gather(1, q).start()

        @pl.when(q < 8)
        def _():
            over_x((q + 2 * (1 - l)) % 4).wait_recv()

        for r in range(2):
            @pl.when((q >= 8) & (q < 12))
            def _():
                in_y(r, (q - 8) % 2 + jnp.where(q < 10, 0, 4) + 2 * r).wait_recv()

            @pl.when(q < 12)
            def _():
                in_y(r, q).start()

    for r in range(2):
        for n in (2 - 2 * r, 3 - 2 * r, 6 - 2 * r, 7 - 2 * r, 8, 9, 10, 11):
            in_y(r, n).wait_recv()

    def slices(r, q):
        step, u = q // 4, (q + 2 * r) % 4

        def slot(steps):
            return jnp.where(steps == 4, 768, (steps - 1) * SUB + r * 128)

        dst = rec.at[1, at(slot(step + 1) + u * 32, 32)]

        def copy(src):
            return pltpu.make_async_remote_copy(
                src_ref=src, dst_ref=dst, send_sem=slice_send.at[r], recv_sem=slice_recv.at[r, q],
                device_id=lines[r], device_id_type=MESH)

        return copy(own.at[1, at(a * 128 + u * 32, 32)]), copy(rec.at[1, at(slot(jnp.maximum(step, 1)) + u * 32, 32)])

    for q in range(4):
        for r in range(2):
            slices(r, q)[0].start()

    for q in range(10, 14):
        gather(0, q).wait_recv()
        gather(1, q if q >= 12 else q - 2).wait_recv()

    for copy in old_in:
        copy.wait()

    node = ((y - z // 2 + 4) % 4) * 2 + (h + z % 2) % 2
    root = node == 0
    level = [lookup(node, LEVEL[tree]) for tree in range(3)]
    deepest = jnp.maximum(jnp.maximum(level[0], level[1]), level[2])

    def source_row(place):
        return ((place % 16) // 4) * SUB + (place // 16) * 64 + (place % 4) * CHUNK

    @pl.when(root)
    def _():
        @pl.loop(0, 16)
        def _(n):
            pltpu.make_async_copy(
                own.at[0, at((n % 4) * SUB + (n // 4) * 64, 64)], rec.at[0, at(n * 64, 64)], own_sem.at[0]).start()

    def pass_on(tree, n, way, first):
        place = 3 * n + tree
        dst = rec.at[0, at(place * CHUNK, CHUNK)]
        src = own.at[0, at(source_row(place), CHUNK)] if first else dst
        return pltpu.make_async_remote_copy(
            src_ref=src, dst_ref=dst, send_sem=tree_send.at[tree, way], recv_sem=tree_recv.at[tree, n],
            device_id=plane[way], device_id_type=MESH)

    def l_mate(g):
        return pltpu.make_async_remote_copy(
            src_ref=prod_l.at[g, 1 - c], dst_ref=core_l.at[g],
            send_sem=lcore_send.at[g], recv_sem=lcore_recv.at[g], device_id=mate, device_id_type=MESH)

    def l_twin(g):
        return pltpu.make_async_remote_copy(
            src_ref=chip_l.at[g], dst_ref=last_l.at[g],
            send_sem=lchip_send.at[g], recv_sem=lchip_recv.at[g], device_id=twin, device_id_type=MESH)

    def l_out(half):
        cols = pl.ds(half * 128, 128)
        return pltpu.make_async_copy(out.at[0, :, cols], l_ref.at[:, cols], out_sem.at[0, half])

    def l_multiply(g, n):
        tile = lax.dot_general(
            rec[0, at(g * SUB, SUB), :], own[0, at(n * SUB, SUB), :],
            (((1,), (1,)), ((), ())), preferred_element_type=F32)
        for s in range(4):
            prod_l[g, s % 2, s // 2, :, at(n * SUB, SUB)] = tile[s * 64:(s + 1) * 64, :]

        @pl.when(n == 3)
        def _():
            l_mate(g).start()

    def l_add(g):
        l_mate(g).wait_recv()
        chip_l[g] = prod_l[g, c, 1 - l] + core_l[g, 1 - l]
        l_twin(g).start()

    def l_finish(g):
        l_twin(g).wait_recv()
        total[at(g * 64, 64), :] = prod_l[g, c, l] + core_l[g, l] + last_l[g]
        for half in range(2):
            @pl.when(g == 2 * half + 1)
            def _():
                cols = slice(half * 128, (half + 1) * 128)
                for n in range(4):
                    rows = slice(n * 256, (n + 1) * 256)
                    out[0, rows, cols] = 0.95 * old[0, rows, cols] + 0.05 * total[cols, rows].T
                l_out(half).start()

    def r_mate(g, size):
        rows = pl.ds(0, size)
        return pltpu.make_async_remote_copy(
            src_ref=prod_r.at[g, 1 - c, :, rows], dst_ref=core_r.at[g, :, rows],
            send_sem=rcore_send.at[g], recv_sem=rcore_recv.at[g], device_id=mate, device_id_type=MESH)

    def r_twin(g, size):
        rows = pl.ds(0, size)
        return pltpu.make_async_remote_copy(
            src_ref=chip_r.at[g, rows], dst_ref=last_r.at[g, rows],
            send_sem=rchip_send.at[g], recv_sem=rchip_recv.at[g], device_id=twin, device_id_type=MESH)

    def r_multiply(g, size, operand, step):
        s_c, s_l = (1 - c + step // 2) % 2, step % 2
        prod_r[g, s_c, s_l, 0:size] = lax.dot_general(
            operand[...], own[1, at((s_l * 2 + s_c) * SUB, SUB), :],
            (((1,), (1,)), ((), ())), preferred_element_type=F32)

        @pl.when(step == 1)
        def _():
            r_mate(g, size).start()

    def kept_l(g):
        return (l + h + z + (jnp.where(g < FAR, g + 1, 0) if not isinstance(g, int) else 0)) % 2

    def r_add(g, size):
        r_mate(g, size).wait_recv()
        chip_r[g, 0:size] = prod_r[g, c, 1 - kept_l(g), 0:size] + core_r[g, 1 - kept_l(g), 0:size]
        r_twin(g, size).start()

    def home(g, part):
        if isinstance(g, int):
            b = (z + (4 if g == FAR else 0)) % RING
        else:
            b = (z + (2 * part - 1) * (g + 1) + RING) % RING
        src, dst = sum_r.at[g, pl.ds(part * 128, 128)], stage.at[a]
        here = pltpu.make_async_copy(src, dst, home_recv.at[a])
        away = pltpu.make_async_remote_copy(
            src_ref=src, dst_ref=dst, send_sem=home_send.at[g, part], recv_sem=home_recv.at[a],
            device_id=in_plane(b), device_id_type=MESH)
        return b, here, away

    def r_finish(g, size):
        r_twin(g, size).wait_recv()
        sum_r[g, 0:size] = prod_r[g, c, kept_l(g), 0:size] + core_r[g, kept_l(g), 0:size] + last_r[g, 0:size]
        for part in range(size // 128):
            b, here, away = home(g, part)

            @pl.when(b == a)
            def _():
                here.start()

            @pl.when(b != a)
            def _():
                away.start()

    def r_out(n):
        rows = pl.ds(n * 128, 128)
        return pltpu.make_async_copy(out.at[1, rows], r_ref.at[rows], out_sem.at[1, n])

    @pl.loop(0, 47)
    def _(t):
        for tree in range(3):
            n = t - LAG * level[tree]

            @pl.when((n >= 0) & (n < COUNT[tree]))
            def _():
                @pl.when(root)
                def _():
                    pass_on(tree, n, tree, True).start()

                @pl.when(node > 0)
                def _():
                    pass_on(tree, n, 0, False).wait_recv()

                for way in range(3):
                    senders = tuple(v for v in ONWARD[tree][way] if v > 0)
                    if senders:
                        @pl.when(one_of(node, senders))
                        def _():
                            pass_on(tree, n, way, False).start()

        q = t // 2

        @pl.when(t % 2 == 0)
        def _():
            @pl.when((q >= 4) & (q < 18))
            def _():
                for r in range(2):
                    slices(r, q - 4)[0].wait_recv()

                    @pl.when(q < 14)
                    def _():
                        slices(r, q)[1].start()

        n = t - LAG * deepest

        @pl.when(root & (t == READY[0]))
        def _():
            pltpu.make_async_copy(own.at[0], rec.at[0], own_sem.at[0]).wait()

        for ready in READY:
            @pl.when((n >= ready) & (n < ready + 4))
            def _():
                l_multiply(READY.index(ready), n - ready)

        @pl.when(one_of(n - ADD, READY))
        def _():
            l_add((n - ADD) // 5 - 1)

        @pl.when(one_of(n - END, READY))
        def _():
            l_finish((n - END) // 5 - 1)

        @pl.when((t >= 2) & (t < 6))
        def _():
            r_multiply(HERE, 128, own.at[1, at(a * 128, 128)], t - 2)

        @pl.when(t == 6)
        def _():
            r_add(HERE, 128)

        @pl.when(t == 11)
        def _():
            r_finish(HERE, 128)

        m = t - 15

        @pl.when((m >= 0) & (m < 24) & (m % 8 < 4))
        def _():
            g = m // 8
            r_multiply(g, 256, rec.at[1, at(g * SUB, SUB)], m % 8)

        @pl.when((m >= 0) & (m < 24) & (m % 8 == 4))
        def _():
            r_add(m // 8, 256)

        @pl.when((m >= 9) & (m < 32) & (m % 8 == 1))
        def _():
            r_finish(m // 8 - 1, 256)

        @pl.when(t == 36)
        def _():
            @pl.loop(0, 4)
            def _(step):
                r_multiply(FAR, 128, rec.at[1, pl.ds(768, 128)], step)

        @pl.when(t == 37)
        def _():
            r_add(FAR, 128)

        @pl.when(t == 41)
        def _():
            r_finish(FAR, 128)

    for n in range(RING):
        rows = slice(n * 128, (n + 1) * 128)
        pltpu.make_async_copy(stage.at[n], stage.at[n], home_recv.at[n]).wait()
        out[1, rows, :] = 0.95 * old[1, rows, :] + 0.05 * stage[n]
        r_out(n).start()

    def sent(ref, sem):
        pltpu.make_async_copy(ref, ref, sem).wait()

    for r in range(2):
        sent(own.at[0, pl.ds(0, 448)], line_send.at[r])
        sent(own.at[1, pl.ds(0, 384)], y_send.at[r])
        sent(own.at[1, pl.ds(0, 448)], slice_send.at[r])
    sent(own.at[1, pl.ds(0, 128)], x_send.at[0])
    for tree in range(3):
        for way in range(3):
            if ONWARD[tree][way]:
                @pl.when(one_of(node, ONWARD[tree][way]))
                def _():
                    sent(rec.at[0, pl.ds(0, COUNT[tree] * CHUNK)], tree_send.at[tree, way])
    for u in range(2):
        swap(u).wait_send()
    for dl, dc in ((1, 0), (1, 1), (0, 1)):
        mix(dl, dc).wait_send()
    for g in range(4):
        l_mate(g).wait_send()
        l_twin(g).wait_send()
    for g in range(5):
        size = 256 if g < 3 else 128
        r_mate(g, size).wait_send()
        r_twin(g, size).wait_send()
        for part in range(size // 128):
            b, here, away = home(jnp.int32(g) if g < 3 else g, part)

            @pl.when(b != a)
            def _():
                away.wait_send()
    for half in range(2):
        l_out(half).wait()
    for n in range(RING):
        r_out(n).wait()


def on_device(gradient, left_old, right_old):
    factor = jax.ShapeDtypeStruct((ROW, SUB), F32)
    anywhere = pl.BlockSpec(memory_space=pl.ANY)
    dma = pltpu.SemaphoreType.DMA
    return pl.pallas_call(
        kernel,
        out_shape=(factor, factor),
        in_specs=[anywhere] * 3,
        out_specs=(anywhere, anywhere),
        scratch_shapes=[
            pltpu.VMEM((ROW, SUB), BF16), pltpu.VMEM((SUB, ROW), BF16),
            pltpu.VMEM((2, ROW, DEPTH), BF16), pltpu.VMEM((2, ROW, DEPTH), BF16),
            pltpu.VMEM((4, 2, 2, 64, ROW), F32), pltpu.VMEM((4, 2, 64, ROW), F32), pltpu.VMEM((4, 64, ROW), F32),
            pltpu.VMEM((4, 64, ROW), F32), pltpu.VMEM((SUB, ROW), F32),
            pltpu.VMEM((5, 2, 2, SUB, SUB), F32), pltpu.VMEM((5, 2, SUB, SUB), F32), pltpu.VMEM((5, SUB, SUB), F32),
            pltpu.VMEM((5, SUB, SUB), F32), pltpu.VMEM((5, SUB, SUB), F32), pltpu.VMEM((RING, 128, SUB), F32),
            pltpu.VMEM((2, ROW, SUB), F32), pltpu.VMEM((2, ROW, SUB), F32),
            dma((3,)), dma((2,)), dma((4,)), dma((4,)), dma((4,)), dma((2,)), dma((2, 14)), dma((1,)), dma((4,)), dma((2,)),
            dma((2, 12)), dma((2,)), dma((2, 14)), dma((3, 3)), dma((3, 22)), dma((1,)),
            dma((4,)), dma((4,)), dma((4,)), dma((4,)), dma((5,)), dma((5,)), dma((5,)), dma((5,)),
            dma((5, 2)), dma((RING,)), dma((2, RING)),
        ],
        compiler_params=pltpu.CompilerParams(collective_id=0, has_side_effects=True, vmem_limit_bytes=56 << 20),
        cost_estimate=pl.CostEstimate(flops=4 * ROW * SUB * 8192, bytes_accessed=5 << 20, transcendentals=0),
        name="gram_factors",
    )(gradient, left_old, right_old)


def solution(mesh):
    placed = (P("row", "col"), P("row", "col"), P("row", "col"))
    return jax.shard_map(
        on_device,
        mesh=mesh,
        in_specs=placed,
        out_specs=(P("row", "col"), P("row", "col")),
        check_vma=False,
    )
```

```python
import jax
import jax.numpy as jnp
from jax import lax
from jax.experimental import pallas as pl
from jax.experimental.pallas import tpu as pltpu
from jax.sharding import PartitionSpec as P

MESH = pl.DeviceIdType.MESH
BF16, F32 = jnp.bfloat16, jnp.float32
ROW = 1024
SUB = 256
RING = 8
DEPTH = RING * SUB
CHUNK = 16
COUNT = (22, 21, 21)
HOME = 23
START = 0
LAG = 4
ADD, END = 4, 9
READY = (5, 10, 15, 21)
LEVEL = ((0, 3, 1, 2, 2, 3, 3, 4), (0, 3, 3, 4, 2, 3, 1, 2), (0, 1, 3, 2, 4, 3, 3, 2))
ONWARD = (((0, 2, 4, 5), (3,), (2, 4)), ((7,), (0, 6, 4, 7, 5), (6,)), ((1, 3), (1,), (0, 3, 7, 5)))
FAR, HERE = 3, 5
SIZES, PARTS = (256, 256, 256, 64, 64, 128), (2, 2, 2, 2, 2, 1)


def at(start, size):
    return pl.ds(pl.multiple_of(start, size), size)


def one_of(value, choices):
    found = value == choices[0]
    for choice in choices[1:]:
        found = found | (value == choice)
    return found


def lookup(index, values):
    result = jnp.int32(0)
    for place, value in enumerate(values):
        result = result + jnp.where(index == place, value, 0)
    return result


def kernel(g_ref, l_ref, r_ref,
           grad, turned, own, rec, prod_l, core_l, chip_l, last_l, total, prod_r, core_r, chip_r, last_r, sum_r, out,
           load_sem, swap_send, swap_recv, mix_send, mix_recv, line_send, line_recv, x_send, x_recv, y_send, y_recv,
           slice_send, slice_recv, tree_send, tree_recv, own_sem,
           lcore_send, lcore_recv, lchip_send, lchip_recv, rcore_send, rcore_recv, rchip_send, rchip_recv,
           home_send, home_recv, out_sem):
    a, j = lax.axis_index("row"), lax.axis_index("col")
    y, h = a // 2, a % 2
    z, l, c = j // 4, (j // 2) % 2, j % 2
    mine = l * 2 + c

    def line(step):
        return (a, ((z + step + RING) % RING) * 4 + mine)

    def along_y(step):
        return (((y + step + 4) % 4) * 2 + h, j)

    def inside(dl, dc):
        return (a, z * 4 + ((l + dl) % 2) * 2 + (c + dc) % 2)

    def in_plane(row):
        return (row, z * 4 + ((l + h + row) % 2) * 2 + c)

    lines = (line(1), line(-1))
    mate, twin = inside(0, 1), inside(1, 0)
    across = (y * 2 + 1 - h, z * 4 + (1 - l) * 2 + c)
    plane = (along_y(1), along_y(-1), across)

    grad_in = pltpu.make_async_copy(g_ref, grad, load_sem.at[0])
    grad_in.start()

    def kept(u):
        rows = pl.ds(u * 512, 512)
        return pltpu.make_async_copy(
            g_ref.at[rows, at(h * 128, 128)], own.at[0, rows, at(z * SUB + h * 128, 128)], swap_recv.at[u])

    def swap(u):
        rows = pl.ds(u * 512, 512)
        return pltpu.make_async_remote_copy(
            src_ref=g_ref.at[rows, at((1 - h) * 128, 128)], dst_ref=own.at[0, rows, at(z * SUB + (1 - h) * 128, 128)],
            send_sem=swap_send.at[u], recv_sem=swap_recv.at[2 + u], device_id=twin, device_id_type=MESH)

    kept(0).start()
    kept(1).start()

    barrier = pltpu.get_barrier_semaphore()
    for device in lines + (mate, twin, inside(1, 1)):
        pl.semaphore_signal(barrier, inc=1, device_id=device, device_id_type=MESH)
    for step in range(1, RING):
        pl.semaphore_signal(barrier, inc=1, device_id=in_plane((a + step) % RING), device_id_type=MESH)
    pl.semaphore_wait(barrier, 12)

    swap(0).start()
    swap(1).start()

    def gather(r, q):
        step, u = q // 4, q % 4
        if r == 1:
            u = u + jnp.where(step == 3, 2, 0)
        k = (z - (1 - 2 * r) * step + RING) % RING
        side = jnp.where(u < 2, h, 1 - h)
        part = own.at[0, at((u % 2) * 512, 512), at(k * SUB + side * 128, 128)]
        return pltpu.make_async_remote_copy(
            src_ref=part, dst_ref=part, send_sem=line_send.at[r], recv_sem=line_recv.at[r, q],
            device_id=lines[r], device_id_type=MESH)

    for u in range(2):
        kept(u).wait()
        gather(0, u).start()
        gather(1, u).start()

    grad_in.wait()
    for u in range(4):
        turned[:, u * SUB:(u + 1) * SUB] = grad[u * SUB:(u + 1) * SUB, :].T

    def mix(dl, dc):
        part = ((l + dl + h) % 2) * 2 + (c + dc) % 2
        src = turned.at[:, at(part * SUB, SUB)]
        dst = own.at[1, at(mine * SUB, SUB), at(a * SUB, SUB)]
        if dl == dc == 0:
            return pltpu.make_async_copy(src, dst, mix_recv.at[mine])
        return pltpu.make_async_remote_copy(
            src_ref=src, dst_ref=dst, send_sem=mix_send.at[dl * 2 + dc], recv_sem=mix_recv.at[mine],
            device_id=inside(dl, dc), device_id_type=MESH)

    for dl, dc in ((1, 0), (1, 1), (0, 1), (0, 0)):
        mix(dl, dc).start()

    def in_y(r, n):
        late = n >= 8
        kind = jnp.where(late, (n - 8) // 2, n // 4)
        v = jnp.where(late, (n - 8) % 2 + 2 * r, n % 4)
        from_y = (y - jnp.where(late, 1 - 2 * r, 0) + 4) % 4
        k = from_y * 2 + (h + kind) % 2
        u = (v + 2 * ((l + kind) % 2)) % 4
        part = own.at[1, at(u * SUB, SUB), at(k * SUB, SUB)]
        return pltpu.make_async_remote_copy(
            src_ref=part, dst_ref=part, send_sem=y_send.at[r], recv_sem=y_recv.at[r, n],
            device_id=plane[r], device_id_type=MESH)

    def over_x(u):
        part = own.at[1, at(u * SUB, SUB), at(a * SUB, SUB)]
        return pltpu.make_async_remote_copy(
            src_ref=part, dst_ref=part, send_sem=x_send.at[0], recv_sem=x_recv.at[u], device_id=across, device_id_type=MESH)

    for u in range(2):
        swap(u).wait_recv()
        gather(0, 2 + u).start()
        gather(1, 2 + u).start()
    for v in range(4):
        u = (v + 2 * l) % 4
        here = own.at[1, at(u * SUB, SUB), at(a * SUB, SUB)]
        pltpu.make_async_copy(here, here, mix_recv.at[u]).wait()
        over_x(u).start()
        in_y(0, v).start()
        in_y(1, v).start()

    @pl.loop(4, 14)
    def _(q):
        gather(0, q - 4).wait_recv()
        gather(0, q).start()
        gather(1, q - jnp.where(q < 12, 4, 2)).wait_recv()
        gather(1, q).start()

        @pl.when(q < 8)
        def _():
            over_x((q + 2 * (1 - l)) % 4).wait_recv()

        for r in range(2):
            @pl.when((q >= 8) & (q < 12))
            def _():
                in_y(r, (q - 8) % 2 + jnp.where(q < 10, 0, 4) + 2 * r).wait_recv()

            @pl.when(q < 12)
            def _():
                in_y(r, q).start()

    for r in range(2):
        for n in (2 - 2 * r, 3 - 2 * r, 6 - 2 * r, 7 - 2 * r, 8, 9, 10, 11):
            in_y(r, n).wait_recv()

    def slices(r, q):
        step, u = q // 4, (q + 2 * r) % 4

        def slot(steps):
            return (steps - 1) * SUB + r * 128 + u * 32

        dst = rec.at[1, at(jnp.where(step == 3, 768 + (q % 4) * 64 + r * 32, slot(step + 1)), 32)]

        def copy(src):
            return pltpu.make_async_remote_copy(
                src_ref=src, dst_ref=dst, send_sem=slice_send.at[r], recv_sem=slice_recv.at[r, q],
                device_id=lines[r], device_id_type=MESH)

        return copy(own.at[1, at(a * 128 + u * 32, 32)]), copy(rec.at[1, at(slot(jnp.maximum(step, 1)), 32)])

    for q in range(4):
        for r in range(2):
            slices(r, q)[0].start()

    for q in range(10, 14):
        gather(0, q).wait_recv()
        gather(1, q if q >= 12 else q - 2).wait_recv()

    node = ((y - z // 2 + 4) % 4) * 2 + (h + z % 2) % 2
    root = node == 0
    level = [lookup(node, LEVEL[tree]) for tree in range(3)]
    deepest = jnp.maximum(jnp.maximum(level[0], level[1]), level[2])

    def source_row(place):
        return ((place % 16) // 4) * SUB + (place // 16) * 64 + (place % 4) * CHUNK

    @pl.when(root)
    def _():
        @pl.loop(0, 16)
        def _(n):
            pltpu.make_async_copy(
                own.at[0, at((n % 4) * SUB + (n // 4) * 64, 64)], rec.at[0, at(n * 64, 64)], own_sem.at[0]).start()

    def pass_on(tree, n, way, first):
        place = 3 * n + tree
        dst = rec.at[0, at(place * CHUNK, CHUNK)]
        src = own.at[0, at(source_row(place), CHUNK)] if first else dst
        return pltpu.make_async_remote_copy(
            src_ref=src, dst_ref=dst, send_sem=tree_send.at[tree, way], recv_sem=tree_recv.at[tree, n],
            device_id=plane[way], device_id_type=MESH)

    def l_mate(g):
        return pltpu.make_async_remote_copy(
            src_ref=prod_l.at[g, 1 - c], dst_ref=core_l.at[g],
            send_sem=lcore_send.at[g], recv_sem=lcore_recv.at[g], device_id=mate, device_id_type=MESH)

    def l_twin(g):
        return pltpu.make_async_remote_copy(
            src_ref=chip_l.at[g], dst_ref=last_l.at[g],
            send_sem=lchip_send.at[g], recv_sem=lchip_recv.at[g], device_id=twin, device_id_type=MESH)

    def l_out(half):
        cols = pl.ds(half * 128, 128)
        return pltpu.make_async_copy(out.at[:, cols], l_ref.at[:, cols], out_sem.at[half])

    def l_multiply(g, n):
        tile = lax.dot_general(
            rec[0, at(g * SUB, SUB), :], own[0, at(n * 512, 512), :],
            (((1,), (1,)), ((), ())), preferred_element_type=F32)
        for s in range(4):
            prod_l[g, s % 2, s // 2, :, at(n * 512, 512)] = tile[s * 64:(s + 1) * 64, :]

        @pl.when(n == 1)
        def _():
            l_mate(g).start()

    def l_add(g):
        l_mate(g).wait_recv()
        chip_l[g] = prod_l[g, c, 1 - l] + core_l[g, 1 - l]
        l_twin(g).start()

    def l_finish(g):
        l_twin(g).wait_recv()
        total[at(g * 64, 64), :] = prod_l[g, c, l] + core_l[g, l] + last_l[g]
        for half in range(2):
            @pl.when(g == 2 * half + 1)
            def _():
                cols = slice(half * 128, (half + 1) * 128)
                for n in range(4):
                    rows = slice(n * 256, (n + 1) * 256)
                    out[rows, cols] = total[cols, rows].T
                l_out(half).start()

    def r_mate(g, size):
        rows = pl.ds(0, size)
        return pltpu.make_async_remote_copy(
            src_ref=prod_r.at[g, 1 - c, :, rows], dst_ref=core_r.at[g, :, rows],
            send_sem=rcore_send.at[g], recv_sem=rcore_recv.at[g], device_id=mate, device_id_type=MESH)

    def r_twin(g, size):
        rows = pl.ds(0, size)
        return pltpu.make_async_remote_copy(
            src_ref=chip_r.at[g, rows], dst_ref=last_r.at[g, rows],
            send_sem=rchip_send.at[g], recv_sem=rchip_recv.at[g], device_id=twin, device_id_type=MESH)

    def r_multiply(g, operand, n):
        tile = lax.dot_general(
            operand[...], own[1, at(n * 512, 512), :], (((1,), (1,)), ((), ())), preferred_element_type=F32)
        for core in range(2):
            prod_r[g, core, n] = tile[:, core * SUB:(core + 1) * SUB]

        @pl.when(n == 1)
        def _():
            r_mate(g, 256).start()

    def r_multiply_few(g, size, operand):
        tile = lax.dot_general(operand[...], own[1], (((1,), (1,)), ((), ())), preferred_element_type=F32)
        for s in range(4):
            prod_r[g, s % 2, s // 2, 0:size] = tile[:, s * SUB:(s + 1) * SUB]
        r_mate(g, size).start()

    def kept_l(g):
        return (l + h + z + (jnp.where(g < FAR, g + 1, 0) if not isinstance(g, int) else 0)) % 2

    def r_add(g, size):
        r_mate(g, size).wait_recv()
        chip_r[g, 0:size] = prod_r[g, c, 1 - kept_l(g), 0:size] + core_r[g, 1 - kept_l(g), 0:size]
        r_twin(g, size).start()

    def home(g, part):
        if isinstance(g, int):
            b, size = (z + (0 if g == HERE else 4)) % RING, 128 if g == HERE else 32
            row = a * 128 + (0 if g == HERE else (2 * part + g - FAR) * 32)
        else:
            b, size, row = (z + (2 * part - 1) * (g + 1) + RING) % RING, 128, a * 128
        src, dst = sum_r.at[g, pl.ds(part * size, size)], r_ref.at[at(row, size)]

        def here():
            return pltpu.make_async_copy(src, dst, home_recv.at[a])

        def away():
            return pltpu.make_async_remote_copy(
                src_ref=src, dst_ref=dst, send_sem=home_send.at[g, part], recv_sem=home_recv.at[a],
                device_id=in_plane(b), device_id_type=MESH)

        return b == a, here, away

    def r_sum(g, size):
        r_twin(g, size).wait_recv()
        sum_r[g, 0:size] = prod_r[g, c, kept_l(g), 0:size] + core_r[g, kept_l(g), 0:size] + last_r[g, 0:size]

    def r_home(g, part):
        stays, here, away = home(g, part)

        @pl.when(stays)
        def _():
            here().start()

        @pl.when(jnp.logical_not(stays))
        def _():
            away().start()

    @pl.loop(0, 48)
    def _(t):
        for tree in range(3):
            n = t - LAG * level[tree] - START

            @pl.when((n >= 0) & (n < COUNT[tree]))
            def _():
                @pl.when(root)
                def _():
                    pass_on(tree, n, tree, True).start()

                @pl.when(node > 0)
                def _():
                    pass_on(tree, n, 0, False).wait_recv()

                for way in range(3):
                    senders = tuple(v for v in ONWARD[tree][way] if v > 0)
                    if senders:
                        @pl.when(one_of(node, senders))
                        def _():
                            pass_on(tree, n, way, False).start()

        q = t // 2

        @pl.when(t % 2 == 0)
        def _():
            @pl.when((q >= 4) & (q < 18))
            def _():
                for r in range(2):
                    slices(r, q - 4)[0].wait_recv()

                    @pl.when(q < 14)
                    def _():
                        slices(r, q)[1].start()

        m = t - 15

        @pl.when((m >= 3) & (m < 24) & (m % 8 == 3))
        def _():
            r_add(m // 8, 256)

        for far in range(2):
            @pl.when(t == 34 + 2 * far)
            def _():
                r_add(FAR + far, 64)

        @pl.when((m >= 7) & (m < 31) & (m % 8 == 7))
        def _():
            r_sum(m // 8, 256)

        for part in range(2):
            g = (t - HOME) // 8

            @pl.when((t >= HOME) & (t < HOME + 24) & ((t - HOME) % 8 == 0))
            def _():
                r_home(g, part)

        for far in range(2):
            @pl.when(t == 39 + far)
            def _():
                r_sum(FAR + far, 64)
                r_home(FAR + far, 0)
                r_home(FAR + far, 1)

        @pl.when((m >= 0) & (m < 24) & (m % 8 < 2))
        def _():
            r_multiply(m // 8, rec.at[1, at((m // 8) * SUB, SUB)], m % 8)

        for far in range(2):
            @pl.when(t == 33 + 2 * far)
            def _():
                r_multiply_few(FAR + far, 64, rec.at[1, pl.ds(768 + 64 * far, 64)])

        @pl.when(t == 2)
        def _():
            r_multiply_few(HERE, 128, own.at[1, at(a * 128, 128)])

        @pl.when(t == 5)
        def _():
            r_add(HERE, 128)

        @pl.when(t == 9)
        def _():
            r_sum(HERE, 128)
            r_home(HERE, 0)

        n = t - LAG * deepest - START

        @pl.when(root & (n == READY[0]))
        def _():
            pltpu.make_async_copy(own.at[0], rec.at[0], own_sem.at[0]).wait()

        for ready in READY:
            @pl.when((n >= ready) & (n < ready + 2))
            def _():
                l_multiply(READY.index(ready), n - ready)

        @pl.when(one_of(n - ADD, READY))
        def _():
            l_add((n - ADD) // 5 - 1)

        @pl.when(one_of(n - END, READY))
        def _():
            l_finish((n - END) // 5 - 1)


    for n in range(RING):
        rows = r_ref.at[pl.ds(n * 128, 128)]
        pltpu.make_async_copy(rows, rows, home_recv.at[n]).wait()

    def sent(ref, sem):
        pltpu.make_async_copy(ref, ref, sem).wait()

    for r in range(2):
        sent(own.at[0, pl.ds(0, 448)], line_send.at[r])
        sent(own.at[1, pl.ds(0, 384)], y_send.at[r])
        sent(own.at[1, pl.ds(0, 448)], slice_send.at[r])
    sent(own.at[1, pl.ds(0, 128)], x_send.at[0])
    for tree in range(3):
        for way in range(3):
            if ONWARD[tree][way]:
                @pl.when(one_of(node, ONWARD[tree][way]))
                def _():
                    sent(rec.at[0, pl.ds(0, COUNT[tree] * CHUNK)], tree_send.at[tree, way])
    for u in range(2):
        swap(u).wait_send()
    for dl, dc in ((1, 0), (1, 1), (0, 1)):
        mix(dl, dc).wait_send()
    for g in range(4):
        l_mate(g).wait_send()
        l_twin(g).wait_send()
    for g in range(6):
        r_mate(g, SIZES[g]).wait_send()
        r_twin(g, SIZES[g]).wait_send()
        for part in range(PARTS[g]):
            stays, here, away = home(jnp.int32(g) if g < FAR else g, part)

            @pl.when(jnp.logical_not(stays))
            def _():
                away().wait_send()
    for half in range(2):
        l_out(half).wait()


def on_device(gradient, left_old, right_old):
    factor = jax.ShapeDtypeStruct((ROW, SUB), F32)
    anywhere = pl.BlockSpec(memory_space=pl.ANY)
    dma = pltpu.SemaphoreType.DMA
    gram_left, gram_right = pl.pallas_call(
        kernel,
        out_shape=(factor, factor),
        in_specs=[anywhere],
        out_specs=(anywhere, anywhere),
        scratch_shapes=[
            pltpu.VMEM((ROW, SUB), BF16), pltpu.VMEM((SUB, ROW), BF16),
            pltpu.VMEM((2, ROW, DEPTH), BF16), pltpu.VMEM((2, ROW, DEPTH), BF16),
            pltpu.VMEM((4, 2, 2, 64, ROW), F32), pltpu.VMEM((4, 2, 64, ROW), F32), pltpu.VMEM((4, 64, ROW), F32),
            pltpu.VMEM((4, 64, ROW), F32), pltpu.VMEM((SUB, ROW), F32),
            pltpu.VMEM((6, 2, 2, SUB, SUB), F32), pltpu.VMEM((6, 2, SUB, SUB), F32), pltpu.VMEM((6, SUB, SUB), F32),
            pltpu.VMEM((6, SUB, SUB), F32), pltpu.VMEM((6, SUB, SUB), F32), pltpu.VMEM((ROW, SUB), F32),
            dma((1,)), dma((2,)), dma((4,)), dma((4,)), dma((4,)), dma((2,)), dma((2, 14)), dma((1,)), dma((4,)), dma((2,)),
            dma((2, 12)), dma((2,)), dma((2, 14)), dma((3, 3)), dma((3, 22)), dma((1,)),
            dma((4,)), dma((4,)), dma((4,)), dma((4,)), dma((6,)), dma((6,)), dma((6,)), dma((6,)),
            dma((6, 2)), dma((RING,)), dma((2,)),
        ],
        compiler_params=pltpu.CompilerParams(collective_id=0, has_side_effects=True, vmem_limit_bytes=56 << 20),
        cost_estimate=pl.CostEstimate(flops=4 * ROW * SUB * 8192, bytes_accessed=5 << 20, transcendentals=0),
        name="gram_factors",
    )(gradient)
    return 0.95 * left_old + 0.05 * gram_left, 0.95 * right_old + 0.05 * gram_right


def solution(mesh):
    placed = (P("row", "col"), P("row", "col"), P("row", "col"))
    return jax.shard_map(
        on_device,
        mesh=mesh,
        in_specs=placed,
        out_specs=(P("row", "col"), P("row", "col")),
        check_vma=False,
    )
```

```python
import jax
import jax.numpy as jnp
from jax import lax
from jax.experimental import pallas as pl
from jax.experimental.pallas import tpu as pltpu
from jax.sharding import PartitionSpec as P

MESH = pl.DeviceIdType.MESH
BF16, F32 = jnp.bfloat16, jnp.float32
ROW = 1024
SUB = 256
RING = 8
DEPTH = RING * SUB
CHUNK = 16
COUNT = (22, 21, 21)
HOME = 23
START = 0
LAG = 4
ADD, END = 3, 9
READY = (5, 10, 15, 21)
LEVEL = ((0, 3, 1, 2, 2, 3, 3, 4), (0, 3, 3, 4, 2, 3, 1, 2), (0, 1, 3, 2, 4, 3, 3, 2))
ONWARD = (((0, 2, 4, 5), (3,), (2, 4)), ((7,), (0, 6, 4, 7, 5), (6,)), ((1, 3), (1,), (0, 3, 7, 5)))
FAR, HERE = 3, 5
SIZES, PARTS = (256, 256, 256, 64, 64, 128), (2, 2, 2, 2, 2, 1)


def at(start, size):
    return pl.ds(pl.multiple_of(start, size), size)


def one_of(value, choices):
    found = value == choices[0]
    for choice in choices[1:]:
        found = found | (value == choice)
    return found


def lookup(index, values):
    result = jnp.int32(0)
    for place, value in enumerate(values):
        result = result + jnp.where(index == place, value, 0)
    return result


def kernel(g_ref, l_ref, r_ref,
           grad, turned, own, rec, prod_l, core_l, chip_l, last_l, total, prod_r, core_r, chip_r, last_r, sum_r, out,
           load_sem, swap_send, swap_recv, mix_send, mix_recv, line_send, line_recv, x_send, x_recv, y_send, y_recv,
           slice_send, slice_recv, tree_send, tree_recv, own_sem,
           lcore_send, lcore_recv, lchip_send, lchip_recv, rcore_send, rcore_recv, rchip_send, rchip_recv,
           home_send, home_recv, out_sem):
    a, j = lax.axis_index("row"), lax.axis_index("col")
    y, h = a // 2, a % 2
    z, l, c = j // 4, (j // 2) % 2, j % 2
    mine = l * 2 + c

    def line(step):
        return (a, ((z + step + RING) % RING) * 4 + mine)

    def along_y(step):
        return (((y + step + 4) % 4) * 2 + h, j)

    def inside(dl, dc):
        return (a, z * 4 + ((l + dl) % 2) * 2 + (c + dc) % 2)

    def in_plane(row):
        return (row, z * 4 + ((l + h + row) % 2) * 2 + c)

    lines = (line(1), line(-1))
    mate, twin = inside(0, 1), inside(1, 0)
    across = (y * 2 + 1 - h, z * 4 + (1 - l) * 2 + c)
    plane = (along_y(1), along_y(-1), across)

    grad_in = pltpu.make_async_copy(g_ref, grad, load_sem.at[0])
    grad_in.start()

    def kept(u):
        rows = pl.ds(u * 512, 512)
        return pltpu.make_async_copy(
            g_ref.at[rows, at(h * 128, 128)], own.at[0, rows, at(z * SUB + h * 128, 128)], swap_recv.at[u])

    def swap(u):
        rows = pl.ds(u * 512, 512)
        return pltpu.make_async_remote_copy(
            src_ref=g_ref.at[rows, at((1 - h) * 128, 128)], dst_ref=own.at[0, rows, at(z * SUB + (1 - h) * 128, 128)],
            send_sem=swap_send.at[u], recv_sem=swap_recv.at[2 + u], device_id=twin, device_id_type=MESH)

    kept(0).start()
    kept(1).start()

    barrier = pltpu.get_barrier_semaphore()
    for device in lines + (mate, twin, inside(1, 1)):
        pl.semaphore_signal(barrier, inc=1, device_id=device, device_id_type=MESH)
    for step in range(1, RING):
        pl.semaphore_signal(barrier, inc=1, device_id=in_plane((a + step) % RING), device_id_type=MESH)
    pl.semaphore_wait(barrier, 12)

    swap(0).start()
    swap(1).start()

    def gather(r, q):
        step, u = q // 4, q % 4
        if r == 1:
            u = u + jnp.where(step == 3, 2, 0)
        k = (z - (1 - 2 * r) * step + RING) % RING
        side = jnp.where(u < 2, h, 1 - h)
        part = own.at[0, at((u % 2) * 512, 512), at(k * SUB + side * 128, 128)]
        return pltpu.make_async_remote_copy(
            src_ref=part, dst_ref=part, send_sem=line_send.at[r], recv_sem=line_recv.at[r, q],
            device_id=lines[r], device_id_type=MESH)

    for u in range(2):
        kept(u).wait()
        gather(0, u).start()
        gather(1, u).start()

    grad_in.wait()
    for u in range(4):
        turned[:, u * SUB:(u + 1) * SUB] = grad[u * SUB:(u + 1) * SUB, :].T

    def mix(dl, dc):
        part = ((l + dl + h) % 2) * 2 + (c + dc) % 2
        src = turned.at[:, at(part * SUB, SUB)]
        dst = own.at[1, at(mine * SUB, SUB), at(a * SUB, SUB)]
        if dl == dc == 0:
            return pltpu.make_async_copy(src, dst, mix_recv.at[mine])
        return pltpu.make_async_remote_copy(
            src_ref=src, dst_ref=dst, send_sem=mix_send.at[dl * 2 + dc], recv_sem=mix_recv.at[mine],
            device_id=inside(dl, dc), device_id_type=MESH)

    for dl, dc in ((1, 0), (1, 1), (0, 1), (0, 0)):
        mix(dl, dc).start()

    def in_y(r, n):
        late = n >= 8
        kind = jnp.where(late, (n - 8) // 2, n // 4)
        v = jnp.where(late, (n - 8) % 2 + 2 * r, n % 4)
        from_y = (y - jnp.where(late, 1 - 2 * r, 0) + 4) % 4
        k = from_y * 2 + (h + kind) % 2
        u = (v + 2 * ((l + kind) % 2)) % 4
        part = own.at[1, at(u * SUB, SUB), at(k * SUB, SUB)]
        return pltpu.make_async_remote_copy(
            src_ref=part, dst_ref=part, send_sem=y_send.at[r], recv_sem=y_recv.at[r, n],
            device_id=plane[r], device_id_type=MESH)

    def over_x(u):
        part = own.at[1, at(u * SUB, SUB), at(a * SUB, SUB)]
        return pltpu.make_async_remote_copy(
            src_ref=part, dst_ref=part, send_sem=x_send.at[0], recv_sem=x_recv.at[u], device_id=across, device_id_type=MESH)

    for u in range(2):
        swap(u).wait_recv()
        gather(0, 2 + u).start()
        gather(1, 2 + u).start()
    for v in range(4):
        u = (v + 2 * l) % 4
        here = own.at[1, at(u * SUB, SUB), at(a * SUB, SUB)]
        pltpu.make_async_copy(here, here, mix_recv.at[u]).wait()
        over_x(u).start()
        in_y(0, v).start()
        in_y(1, v).start()

    @pl.loop(4, 14)
    def _(q):
        gather(0, q - 4).wait_recv()
        gather(0, q).start()
        gather(1, q - jnp.where(q < 12, 4, 2)).wait_recv()
        gather(1, q).start()

        @pl.when(q < 8)
        def _():
            over_x((q + 2 * (1 - l)) % 4).wait_recv()

        for r in range(2):
            @pl.when((q >= 8) & (q < 12))
            def _():
                in_y(r, (q - 8) % 2 + jnp.where(q < 10, 0, 4) + 2 * r).wait_recv()

            @pl.when(q < 12)
            def _():
                in_y(r, q).start()

    def slices(r, q):
        step, u = q // 4, (q + 2 * r) % 4

        def slot(steps):
            return (steps - 1) * SUB + r * 128 + u * 32

        dst = rec.at[1, at(jnp.where(step == 3, 768 + (q % 4) * 64 + r * 32, slot(step + 1)), 32)]

        def copy(src):
            return pltpu.make_async_remote_copy(
                src_ref=src, dst_ref=dst, send_sem=slice_send.at[r], recv_sem=slice_recv.at[r, q],
                device_id=lines[r], device_id_type=MESH)

        return copy(own.at[1, at(a * 128 + u * 32, 32)]), copy(rec.at[1, at(slot(jnp.maximum(step, 1)), 32)])

    for q in range(10, 14):
        gather(0, q).wait_recv()
        gather(1, q if q >= 12 else q - 2).wait_recv()

    node = ((y - z // 2 + 4) % 4) * 2 + (h + z % 2) % 2
    root = node == 0
    level = [lookup(node, LEVEL[tree]) for tree in range(3)]
    deepest = jnp.maximum(jnp.maximum(level[0], level[1]), level[2])

    def source_row(place):
        return ((place % 16) // 4) * SUB + (place // 16) * 64 + (place % 4) * CHUNK

    @pl.when(root)
    def _():
        @pl.loop(0, 16)
        def _(n):
            pltpu.make_async_copy(
                own.at[0, at((n % 4) * SUB + (n // 4) * 64, 64)], rec.at[0, at(n * 64, 64)], own_sem.at[0]).start()

    def pass_on(tree, n, way, first):
        place = 3 * n + tree
        dst = rec.at[0, at(place * CHUNK, CHUNK)]
        src = own.at[0, at(source_row(place), CHUNK)] if first else dst
        return pltpu.make_async_remote_copy(
            src_ref=src, dst_ref=dst, send_sem=tree_send.at[tree, way], recv_sem=tree_recv.at[tree, n],
            device_id=plane[way], device_id_type=MESH)

    def l_mate(g):
        return pltpu.make_async_remote_copy(
            src_ref=prod_l.at[g, 1 - c], dst_ref=core_l.at[g],
            send_sem=lcore_send.at[g], recv_sem=lcore_recv.at[g], device_id=mate, device_id_type=MESH)

    def l_twin(g):
        return pltpu.make_async_remote_copy(
            src_ref=chip_l.at[g], dst_ref=last_l.at[g],
            send_sem=lchip_send.at[g], recv_sem=lchip_recv.at[g], device_id=twin, device_id_type=MESH)

    def l_out(half):
        cols = pl.ds(half * 128, 128)
        return pltpu.make_async_copy(out.at[:, cols], l_ref.at[:, cols], out_sem.at[half])

    def l_multiply(g, n):
        tile = lax.dot_general(
            rec[0, at(g * SUB, SUB), :], own[0, at(n * 512, 512), :],
            (((1,), (1,)), ((), ())), preferred_element_type=F32)
        for s in range(4):
            prod_l[g, s % 2, s // 2, :, at(n * 512, 512)] = tile[s * 64:(s + 1) * 64, :]

        @pl.when(n == 1)
        def _():
            l_mate(g).start()

    def l_add(g):
        l_mate(g).wait_recv()
        chip_l[g] = prod_l[g, c, 1 - l] + core_l[g, 1 - l]
        l_twin(g).start()

    def l_finish(g):
        l_twin(g).wait_recv()
        total[at(g * 64, 64), :] = prod_l[g, c, l] + core_l[g, l] + last_l[g]
        for half in range(2):
            @pl.when(g == 2 * half + 1)
            def _():
                cols = slice(half * 128, (half + 1) * 128)
                for n in range(4):
                    rows = slice(n * 256, (n + 1) * 256)
                    out[rows, cols] = total[cols, rows].T
                l_out(half).start()

    def r_mate(g, size):
        rows = pl.ds(0, size)
        return pltpu.make_async_remote_copy(
            src_ref=prod_r.at[g, 1 - c, :, rows], dst_ref=core_r.at[g, :, rows],
            send_sem=rcore_send.at[g], recv_sem=rcore_recv.at[g], device_id=mate, device_id_type=MESH)

    def r_twin(g, size):
        rows = pl.ds(0, size)
        return pltpu.make_async_remote_copy(
            src_ref=chip_r.at[g, rows], dst_ref=last_r.at[g, rows],
            send_sem=rchip_send.at[g], recv_sem=rchip_recv.at[g], device_id=twin, device_id_type=MESH)

    def r_multiply(g, operand, n):
        tile = lax.dot_general(
            operand[...], own[1, at(n * 512, 512), :], (((1,), (1,)), ((), ())), preferred_element_type=F32)
        for core in range(2):
            prod_r[g, core, n] = tile[:, core * SUB:(core + 1) * SUB]

        @pl.when(n == 1)
        def _():
            r_mate(g, 256).start()

    def r_multiply_few(g, size, operand):
        tile = lax.dot_general(operand[...], own[1], (((1,), (1,)), ((), ())), preferred_element_type=F32)
        for s in range(4):
            prod_r[g, s % 2, s // 2, 0:size] = tile[:, s * SUB:(s + 1) * SUB]
        r_mate(g, size).start()

    def kept_l(g):
        return (l + h + z + (0 if isinstance(g, int) else jnp.where(g < FAR, g + 1, 0))) % 2

    def r_add(g, size):
        r_mate(g, size).wait_recv()
        chip_r[g, 0:size] = prod_r[g, c, 1 - kept_l(g), 0:size] + core_r[g, 1 - kept_l(g), 0:size]
        r_twin(g, size).start()

    def home(g, part):
        if isinstance(g, int):
            b, size = (z + (0 if g == HERE else 4)) % RING, 128 if g == HERE else 32
            row = a * 128 + (0 if g == HERE else (2 * part + g - FAR) * 32)
        else:
            b, size, row = (z + (2 * part - 1) * (g + 1) + RING) % RING, 128, a * 128
        src, dst = sum_r.at[g, pl.ds(part * size, size)], r_ref.at[at(row, size)]

        def here():
            return pltpu.make_async_copy(src, dst, home_recv.at[a])

        def away():
            return pltpu.make_async_remote_copy(
                src_ref=src, dst_ref=dst, send_sem=home_send.at[g, part], recv_sem=home_recv.at[a],
                device_id=in_plane(b), device_id_type=MESH)

        return b == a, here, away

    def r_sum(g, size):
        r_twin(g, size).wait_recv()
        sum_r[g, 0:size] = prod_r[g, c, kept_l(g), 0:size] + core_r[g, kept_l(g), 0:size] + last_r[g, 0:size]

    def r_home(g, part):
        stays, here, away = home(g, part)

        @pl.when(stays)
        def _():
            here().start()

        @pl.when(jnp.logical_not(stays))
        def _():
            away().start()

    @pl.loop(0, 48)
    def _(t):
        for tree in range(3):
            n = t - LAG * level[tree] - START

            @pl.when((n >= 0) & (n < COUNT[tree]))
            def _():
                @pl.when(root)
                def _():
                    pass_on(tree, n, tree, True).start()

                @pl.when(node > 0)
                def _():
                    pass_on(tree, n, 0, False).wait_recv()

                for way in range(3):
                    senders = tuple(v for v in ONWARD[tree][way] if v > 0)
                    if senders:
                        @pl.when(one_of(node, senders))
                        def _():
                            pass_on(tree, n, way, False).start()

        @pl.when(t == 0)
        def _():
            for r in range(2):
                for n in (2 - 2 * r, 3 - 2 * r, 6 - 2 * r, 7 - 2 * r, 8, 9, 10, 11):
                    in_y(r, n).wait_recv()
            for q in range(4):
                for r in range(2):
                    slices(r, q)[0].start()

        q = t // 2

        @pl.when(t % 2 == 0)
        def _():
            @pl.when((q >= 4) & (q < 18))
            def _():
                for r in range(2):
                    slices(r, q - 4)[0].wait_recv()

                    @pl.when(q < 14)
                    def _():
                        slices(r, q)[1].start()

        m = t - 15

        @pl.when((m >= 3) & (m < 24) & (m % 8 == 3))
        def _():
            r_add(m // 8, 256)

        @pl.when((t == 34) | (t == 36))
        def _():
            r_add(FAR + (t - 34) // 2, 64)

        @pl.when((m >= 7) & (m < 31) & (m % 8 == 7))
        def _():
            r_sum(m // 8, 256)

        for part in range(2):
            g = (t - HOME) // 8

            @pl.when((t >= HOME) & (t < HOME + 24) & ((t - HOME) % 8 == 0))
            def _():
                r_home(g, part)

        for far in range(2):
            @pl.when(t == 41 + far)
            def _():
                r_sum(FAR + far, 64)
                r_home(FAR + far, 0)
                r_home(FAR + far, 1)

        @pl.when((m >= 0) & (m < 24) & (m % 8 < 2))
        def _():
            r_multiply(m // 8, rec.at[1, at((m // 8) * SUB, SUB)], m % 8)

        @pl.when((t == 33) | (t == 35))
        def _():
            far = (t - 33) // 2
            r_multiply_few(FAR + far, 64, rec.at[1, at(768 + 64 * far, 64)])

        @pl.when(t == 2)
        def _():
            r_multiply_few(HERE, 128, own.at[1, at(a * 128, 128)])

        @pl.when(t == 5)
        def _():
            r_add(HERE, 128)

        @pl.when(t == 9)
        def _():
            r_sum(HERE, 128)
            r_home(HERE, 0)

        n = t - LAG * deepest - START

        @pl.when(root & (n == READY[0]))
        def _():
            pltpu.make_async_copy(own.at[0], rec.at[0], own_sem.at[0]).wait()

        group = sum((n >= ready).astype(jnp.int32) for ready in READY[1:])
        since = n - lookup(group, READY)

        @pl.when((since >= 0) & (since < 2))
        def _():
            l_multiply(group, since)

        @pl.when(one_of(n - ADD, READY))
        def _():
            l_add((n - ADD) // 5 - 1)

        @pl.when(one_of(n - END, READY))
        def _():
            l_finish((n - END) // 5 - 1)


    for n in range(RING):
        rows = r_ref.at[pl.ds(n * 128, 128)]
        pltpu.make_async_copy(rows, rows, home_recv.at[n]).wait()

    def sent(ref, sem):
        pltpu.make_async_copy(ref, ref, sem).wait()

    for r in range(2):
        sent(own.at[0, pl.ds(0, 448)], line_send.at[r])
        sent(own.at[1, pl.ds(0, 384)], y_send.at[r])
        sent(own.at[1, pl.ds(0, 448)], slice_send.at[r])
    sent(own.at[1, pl.ds(0, 128)], x_send.at[0])
    for tree in range(3):
        for way in range(3):
            if ONWARD[tree][way]:
                @pl.when(one_of(node, ONWARD[tree][way]))
                def _():
                    sent(rec.at[0, pl.ds(0, COUNT[tree] * CHUNK)], tree_send.at[tree, way])
    for u in range(2):
        swap(u).wait_send()
    for dl, dc in ((1, 0), (1, 1), (0, 1)):
        mix(dl, dc).wait_send()
    for g in range(4):
        l_mate(g).wait_send()
        l_twin(g).wait_send()
    for g in range(6):
        r_mate(g, SIZES[g]).wait_send()
        r_twin(g, SIZES[g]).wait_send()
        for part in range(PARTS[g]):
            stays, here, away = home(jnp.int32(g) if g < FAR else g, part)

            @pl.when(jnp.logical_not(stays))
            def _():
                away().wait_send()
    for half in range(2):
        l_out(half).wait()


def on_device(gradient, left_old, right_old):
    factor = jax.ShapeDtypeStruct((ROW, SUB), F32)
    anywhere = pl.BlockSpec(memory_space=pl.ANY)
    dma = pltpu.SemaphoreType.DMA
    gram_left, gram_right = pl.pallas_call(
        kernel,
        out_shape=(factor, factor),
        in_specs=[anywhere],
        out_specs=(anywhere, anywhere),
        scratch_shapes=[
            pltpu.VMEM((ROW, SUB), BF16), pltpu.VMEM((SUB, ROW), BF16),
            pltpu.VMEM((2, ROW, DEPTH), BF16), pltpu.VMEM((2, ROW, DEPTH), BF16),
            pltpu.VMEM((4, 2, 2, 64, ROW), F32), pltpu.VMEM((4, 2, 64, ROW), F32), pltpu.VMEM((4, 64, ROW), F32),
            pltpu.VMEM((4, 64, ROW), F32), pltpu.VMEM((SUB, ROW), F32),
            pltpu.VMEM((6, 2, 2, SUB, SUB), F32), pltpu.VMEM((6, 2, SUB, SUB), F32), pltpu.VMEM((6, SUB, SUB), F32),
            pltpu.VMEM((6, SUB, SUB), F32), pltpu.VMEM((6, SUB, SUB), F32), pltpu.VMEM((ROW, SUB), F32),
            dma((1,)), dma((2,)), dma((4,)), dma((4,)), dma((4,)), dma((2,)), dma((2, 14)), dma((1,)), dma((4,)), dma((2,)),
            dma((2, 12)), dma((2,)), dma((2, 14)), dma((3, 3)), dma((3, 22)), dma((1,)),
            dma((4,)), dma((4,)), dma((4,)), dma((4,)), dma((6,)), dma((6,)), dma((6,)), dma((6,)),
            dma((6, 2)), dma((RING,)), dma((2,)),
        ],
        compiler_params=pltpu.CompilerParams(collective_id=0, has_side_effects=True, vmem_limit_bytes=56 << 20),
        cost_estimate=pl.CostEstimate(flops=4 * ROW * SUB * 8192, bytes_accessed=5 << 20, transcendentals=0),
        name="gram_factors",
    )(gradient)
    return 0.95 * left_old + 0.05 * gram_left, 0.95 * right_old + 0.05 * gram_right


def solution(mesh):
    placed = (P("row", "col"), P("row", "col"), P("row", "col"))
    return jax.shard_map(
        on_device,
        mesh=mesh,
        in_specs=placed,
        out_specs=(P("row", "col"), P("row", "col")),
        check_vma=False,
    )
```

```python
import jax
import jax.numpy as jnp
from jax import lax
from jax.experimental import pallas as pl
from jax.experimental.pallas import tpu as pltpu
from jax.sharding import PartitionSpec as P

MESH = pl.DeviceIdType.MESH
BF16, F32 = jnp.bfloat16, jnp.float32
ROW = 1024
SUB = 256
RING = 8
DEPTH = RING * SUB
CHUNK = 16
COUNT = (22, 21, 21)
HOME = 23
START = 0
LAG = 4
ADD, END = 3, 9
READY = (5, 10, 15, 21)
LEVEL = ((0, 3, 1, 2, 2, 3, 3, 4), (0, 3, 3, 4, 2, 3, 1, 2), (0, 1, 3, 2, 4, 3, 3, 2))
ONWARD = (((0, 2, 4, 5), (3,), (2, 4)), ((7,), (0, 6, 4, 7, 5), (6,)), ((1, 3), (1,), (0, 3, 7, 5)))
FAR, HERE = 3, 5
SIZES, PARTS = (256, 256, 256, 64, 64, 128), (2, 2, 2, 2, 2, 1)


def at(start, size):
    return pl.ds(pl.multiple_of(start, size), size)


def one_of(value, choices):
    found = value == choices[0]
    for choice in choices[1:]:
        found = found | (value == choice)
    return found


def lookup(index, values):
    result = jnp.int32(0)
    for place, value in enumerate(values):
        result = result + jnp.where(index == place, value, 0)
    return result


def kernel(g_ref, l_ref, r_ref,
           grad, turned, own, rec, prod_l, core_l, chip_l, last_l, total, prod_r, core_r, chip_r, last_r, sum_r, out,
           load_sem, swap_send, swap_recv, mix_send, mix_recv, line_send, line_recv, x_send, x_recv, y_send, y_recv,
           slice_send, slice_recv, tree_send, tree_recv, own_sem,
           lcore_send, lcore_recv, lchip_send, lchip_recv, rcore_send, rcore_recv, rchip_send, rchip_recv,
           home_send, home_recv, out_sem):
    a, j = lax.axis_index("row"), lax.axis_index("col")
    y, h = a // 2, a % 2
    z, l, c = j // 4, (j // 2) % 2, j % 2
    mine = l * 2 + c

    def line(step):
        return (a, ((z + step + RING) % RING) * 4 + mine)

    def along_y(step):
        return (((y + step + 4) % 4) * 2 + h, j)

    def inside(dl, dc):
        return (a, z * 4 + ((l + dl) % 2) * 2 + (c + dc) % 2)

    def in_plane(row):
        return (row, z * 4 + ((l + h + row) % 2) * 2 + c)

    lines = (line(1), line(-1))
    mate, twin = inside(0, 1), inside(1, 0)
    across = (y * 2 + 1 - h, z * 4 + (1 - l) * 2 + c)
    plane = (along_y(1), along_y(-1), across)

    grad_in = pltpu.make_async_copy(g_ref, grad, load_sem.at[0])
    grad_in.start()

    def kept(u):
        rows = pl.ds(u * 512, 512)
        return pltpu.make_async_copy(
            g_ref.at[rows, at(h * 128, 128)], own.at[0, rows, at(z * SUB + h * 128, 128)], swap_recv.at[u])

    def swap(u):
        rows = pl.ds(u * 512, 512)
        return pltpu.make_async_remote_copy(
            src_ref=g_ref.at[rows, at((1 - h) * 128, 128)], dst_ref=own.at[0, rows, at(z * SUB + (1 - h) * 128, 128)],
            send_sem=swap_send.at[u], recv_sem=swap_recv.at[2 + u], device_id=twin, device_id_type=MESH)

    kept(0).start()
    kept(1).start()

    barrier = pltpu.get_barrier_semaphore()
    for device in lines + (mate, twin, inside(1, 1)):
        pl.semaphore_signal(barrier, inc=1, device_id=device, device_id_type=MESH)
    for step in range(1, RING):
        pl.semaphore_signal(barrier, inc=1, device_id=in_plane((a + step) % RING), device_id_type=MESH)
    pl.semaphore_wait(barrier, 12)

    swap(0).start()
    swap(1).start()

    def gather(r, q):
        step, u = q // 4, q % 4
        if r == 1:
            u = u + jnp.where(step == 3, 2, 0)
        k = (z - (1 - 2 * r) * step + RING) % RING
        side = jnp.where(u < 2, h, 1 - h)
        part = own.at[0, at((u % 2) * 512, 512), at(k * SUB + side * 128, 128)]
        return pltpu.make_async_remote_copy(
            src_ref=part, dst_ref=part, send_sem=line_send.at[r], recv_sem=line_recv.at[r, q],
            device_id=lines[r], device_id_type=MESH)

    for u in range(2):
        kept(u).wait()
        gather(0, u).start()
        gather(1, u).start()

    grad_in.wait()
    for u in range(4):
        turned[:, u * SUB:(u + 1) * SUB] = grad[u * SUB:(u + 1) * SUB, :].T

    def mix(dl, dc):
        part = ((l + dl + h) % 2) * 2 + (c + dc) % 2
        src = turned.at[:, at(part * SUB, SUB)]
        dst = own.at[1, at(mine * SUB, SUB), at(a * SUB, SUB)]
        if dl == dc == 0:
            return pltpu.make_async_copy(src, dst, mix_recv.at[mine])
        return pltpu.make_async_remote_copy(
            src_ref=src, dst_ref=dst, send_sem=mix_send.at[dl * 2 + dc], recv_sem=mix_recv.at[mine],
            device_id=inside(dl, dc), device_id_type=MESH)

    for dl, dc in ((1, 0), (1, 1), (0, 1), (0, 0)):
        mix(dl, dc).start()

    def in_y(r, n):
        late = n >= 8
        kind = jnp.where(late, (n - 8) // 2, n // 4)
        v = jnp.where(late, (n - 8) % 2 + 2 * r, n % 4)
        from_y = (y - jnp.where(late, 1 - 2 * r, 0) + 4) % 4
        k = from_y * 2 + (h + kind) % 2
        u = (v + 2 * ((l + kind) % 2)) % 4
        part = own.at[1, at(u * SUB, SUB), at(k * SUB, SUB)]
        return pltpu.make_async_remote_copy(
            src_ref=part, dst_ref=part, send_sem=y_send.at[r], recv_sem=y_recv.at[r, n],
            device_id=plane[r], device_id_type=MESH)

    def over_x(u):
        part = own.at[1, at(u * SUB, SUB), at(a * SUB, SUB)]
        return pltpu.make_async_remote_copy(
            src_ref=part, dst_ref=part, send_sem=x_send.at[0], recv_sem=x_recv.at[u], device_id=across, device_id_type=MESH)

    for u in range(2):
        swap(u).wait_recv()
        gather(0, 2 + u).start()
        gather(1, 2 + u).start()
    for v in range(4):
        u = (v + 2 * l) % 4
        here = own.at[1, at(u * SUB, SUB), at(a * SUB, SUB)]
        pltpu.make_async_copy(here, here, mix_recv.at[u]).wait()
        over_x(u).start()
        in_y(0, v).start()
        in_y(1, v).start()

    @pl.loop(4, 14)
    def _(q):
        gather(0, q - 4).wait_recv()
        gather(0, q).start()
        gather(1, q - jnp.where(q < 12, 4, 2)).wait_recv()
        gather(1, q).start()

        @pl.when(q < 8)
        def _():
            over_x((q + 2 * (1 - l)) % 4).wait_recv()

        for r in range(2):
            @pl.when((q >= 8) & (q < 12))
            def _():
                in_y(r, (q - 8) % 2 + jnp.where(q < 10, 0, 4) + 2 * r).wait_recv()

            @pl.when(q < 12)
            def _():
                in_y(r, q).start()

    def slices(r, q):
        step, u = q // 4, (q + 2 * r) % 4

        def slot(steps):
            return (steps - 1) * SUB + r * 128 + u * 32

        dst = rec.at[1, at(jnp.where(step == 3, 768 + (q % 4) * 64 + r * 32, slot(step + 1)), 32)]

        def copy(src):
            return pltpu.make_async_remote_copy(
                src_ref=src, dst_ref=dst, send_sem=slice_send.at[r], recv_sem=slice_recv.at[r, q],
                device_id=lines[r], device_id_type=MESH)

        return copy(own.at[1, at(a * 128 + u * 32, 32)]), copy(rec.at[1, at(slot(jnp.maximum(step, 1)), 32)])

    for q in range(10, 14):
        gather(0, q).wait_recv()
        gather(1, q if q >= 12 else q - 2).wait_recv()

    node = ((y - z // 2 + 4) % 4) * 2 + (h + z % 2) % 2
    root = node == 0
    level = [lookup(node, LEVEL[tree]) for tree in range(3)]
    deepest = jnp.maximum(jnp.maximum(level[0], level[1]), level[2])

    def source_row(place):
        return ((place % 16) // 4) * SUB + (place // 16) * 64 + (place % 4) * CHUNK

    @pl.when(root)
    def _():
        @pl.loop(0, 16)
        def _(n):
            pltpu.make_async_copy(
                own.at[0, at((n % 4) * SUB + (n // 4) * 64, 64)], rec.at[0, at(n * 64, 64)], own_sem.at[0]).start()

    def pass_on(tree, n, way, first):
        place = 3 * n + tree
        dst = rec.at[0, at(place * CHUNK, CHUNK)]
        src = own.at[0, at(source_row(place), CHUNK)] if first else dst
        return pltpu.make_async_remote_copy(
            src_ref=src, dst_ref=dst, send_sem=tree_send.at[tree, way], recv_sem=tree_recv.at[tree, n],
            device_id=plane[way], device_id_type=MESH)

    def l_mate(g):
        return pltpu.make_async_remote_copy(
            src_ref=prod_l.at[g, 1 - c], dst_ref=core_l.at[g],
            send_sem=lcore_send.at[g], recv_sem=lcore_recv.at[g], device_id=mate, device_id_type=MESH)

    def l_twin(g):
        return pltpu.make_async_remote_copy(
            src_ref=chip_l.at[g], dst_ref=last_l.at[g],
            send_sem=lchip_send.at[g], recv_sem=lchip_recv.at[g], device_id=twin, device_id_type=MESH)

    def l_out(half):
        cols = pl.ds(half * 128, 128)
        return pltpu.make_async_copy(out.at[:, cols], l_ref.at[:, cols], out_sem.at[half])

    def l_multiply(g, n):
        tile = lax.dot_general(
            rec[0, at(g * SUB, SUB), :], own[0, at(n * 512, 512), :],
            (((1,), (1,)), ((), ())), preferred_element_type=F32)
        for s in range(4):
            prod_l[g, s % 2, s // 2, :, at(n * 512, 512)] = tile[s * 64:(s + 1) * 64, :]

        @pl.when(n == 1)
        def _():
            l_mate(g).start()

    def l_add(g):
        l_mate(g).wait_recv()
        chip_l[g] = prod_l[g, c, 1 - l] + core_l[g, 1 - l]
        l_twin(g).start()

    def l_finish(g):
        l_twin(g).wait_recv()
        total[at(g * 64, 64), :] = prod_l[g, c, l] + core_l[g, l] + last_l[g]
        for half in range(2):
            @pl.when(g == 2 * half + 1)
            def _():
                cols = slice(half * 128, (half + 1) * 128)
                for n in range(4):
                    rows = slice(n * 256, (n + 1) * 256)
                    out[rows, cols] = total[cols, rows].T
                l_out(half).start()

    def r_mate(g, size):
        rows = pl.ds(0, size)
        return pltpu.make_async_remote_copy(
            src_ref=prod_r.at[g, 1 - c, :, rows], dst_ref=core_r.at[g, :, rows],
            send_sem=rcore_send.at[g], recv_sem=rcore_recv.at[g], device_id=mate, device_id_type=MESH)

    def r_twin(g, size):
        rows = pl.ds(0, size)
        return pltpu.make_async_remote_copy(
            src_ref=chip_r.at[g, rows], dst_ref=last_r.at[g, rows],
            send_sem=rchip_send.at[g], recv_sem=rchip_recv.at[g], device_id=twin, device_id_type=MESH)

    def r_multiply(g, operand, n):
        tile = lax.dot_general(
            operand[...], own[1, at(n * 512, 512), :], (((1,), (1,)), ((), ())), preferred_element_type=F32)
        for core in range(2):
            prod_r[g, core, n] = tile[:, core * SUB:(core + 1) * SUB]

        @pl.when(n == 1)
        def _():
            r_mate(g, 256).start()

    def r_multiply_few(g, size, operand):
        tile = lax.dot_general(operand[...], own[1], (((1,), (1,)), ((), ())), preferred_element_type=F32)
        for s in range(4):
            prod_r[g, s % 2, s // 2, 0:size] = tile[:, s * SUB:(s + 1) * SUB]
        r_mate(g, size).start()

    def kept_l(g):
        return (l + h + z + (0 if isinstance(g, int) else jnp.where(g < FAR, g + 1, 0))) % 2

    def r_add(g, size):
        r_mate(g, size).wait_recv()
        chip_r[g, 0:size] = prod_r[g, c, 1 - kept_l(g), 0:size] + core_r[g, 1 - kept_l(g), 0:size]
        r_twin(g, size).start()

    def home(g, part):
        if isinstance(g, int):
            b, size = (z + (0 if g == HERE else 4)) % RING, 128 if g == HERE else 32
            row = a * 128 + (0 if g == HERE else (2 * part + g - FAR) * 32)
        else:
            b, size, row = (z + (2 * part - 1) * (g + 1) + RING) % RING, 128, a * 128
        src, dst = sum_r.at[g, pl.ds(part * size, size)], r_ref.at[at(row, size)]

        def here():
            return pltpu.make_async_copy(src, dst, home_recv.at[a])

        def away():
            return pltpu.make_async_remote_copy(
                src_ref=src, dst_ref=dst, send_sem=home_send.at[g, part], recv_sem=home_recv.at[a],
                device_id=in_plane(b), device_id_type=MESH)

        return b == a, here, away

    def r_sum(g, size):
        r_twin(g, size).wait_recv()
        sum_r[g, 0:size] = prod_r[g, c, kept_l(g), 0:size] + core_r[g, kept_l(g), 0:size] + last_r[g, 0:size]

    def r_home(g, part):
        stays, here, away = home(g, part)

        @pl.when(stays)
        def _():
            here().start()

        @pl.when(jnp.logical_not(stays))
        def _():
            away().start()

    @pl.loop(0, 48)
    def _(t):
        for tree in range(3):
            n = t - LAG * level[tree] - START

            @pl.when((n >= 0) & (n < COUNT[tree]))
            def _():
                @pl.when(root)
                def _():
                    pass_on(tree, n, tree, True).start()

                @pl.when(node > 0)
                def _():
                    pass_on(tree, n, 0, False).wait_recv()

                for way in range(3):
                    senders = tuple(v for v in ONWARD[tree][way] if v > 0)
                    if senders:
                        @pl.when(one_of(node, senders))
                        def _():
                            pass_on(tree, n, way, False).start()

        @pl.when(t == 0)
        def _():
            for r in range(2):
                for n in (2 - 2 * r, 3 - 2 * r, 6 - 2 * r, 7 - 2 * r, 8, 9, 10, 11):
                    in_y(r, n).wait_recv()
            pass

        q = t // 2

        @pl.when(t % 2 == 0)
        def _():
            @pl.when(q < 4)
            def _():
                for r in range(2):
                    slices(r, q)[0].start()

            @pl.when((q >= 4) & (q < 18))
            def _():
                for r in range(2):
                    slices(r, q - 4)[0].wait_recv()

                    @pl.when(q < 14)
                    def _():
                        slices(r, q)[1].start()

        m = t - 15

        @pl.when((m >= 3) & (m < 24) & (m % 8 == 3))
        def _():
            r_add(m // 8, 256)

        @pl.when((t == 34) | (t == 36))
        def _():
            r_add(FAR + (t - 34) // 2, 64)

        @pl.when((m >= 7) & (m < 31) & (m % 8 == 7))
        def _():
            r_sum(m // 8, 256)

        for part in range(2):
            g = (t - HOME) // 8

            @pl.when((t >= HOME) & (t < HOME + 24) & ((t - HOME) % 8 == 0))
            def _():
                r_home(g, part)

        for far in range(2):
            @pl.when(t == 41 + far)
            def _():
                r_sum(FAR + far, 64)
                r_home(FAR + far, 0)
                r_home(FAR + far, 1)

        @pl.when((m >= 0) & (m < 24) & (m % 8 < 2))
        def _():
            r_multiply(m // 8, rec.at[1, at((m // 8) * SUB, SUB)], m % 8)

        @pl.when((t == 33) | (t == 35))
        def _():
            far = (t - 33) // 2
            r_multiply_few(FAR + far, 64, rec.at[1, at(768 + 64 * far, 64)])

        @pl.when(t == 2)
        def _():
            r_multiply_few(HERE, 128, own.at[1, at(a * 128, 128)])

        @pl.when(t == 5)
        def _():
            r_add(HERE, 128)

        @pl.when(t == 9)
        def _():
            r_sum(HERE, 128)
            r_home(HERE, 0)

        n = t - LAG * deepest - START

        @pl.when(root & (n == READY[0]))
        def _():
            pltpu.make_async_copy(own.at[0], rec.at[0], own_sem.at[0]).wait()

        group = sum((n >= ready).astype(jnp.int32) for ready in READY[1:])
        since = n - lookup(group, READY)

        @pl.when((since >= 0) & (since < 2))
        def _():
            l_multiply(group, since)

        @pl.when(one_of(n - ADD, READY))
        def _():
            l_add((n - ADD) // 5 - 1)

        @pl.when(one_of(n - END, READY))
        def _():
            l_finish((n - END) // 5 - 1)


    for n in range(RING):
        rows = r_ref.at[pl.ds(n * 128, 128)]
        pltpu.make_async_copy(rows, rows, home_recv.at[n]).wait()

    def sent(ref, sem):
        pltpu.make_async_copy(ref, ref, sem).wait()

    for r in range(2):
        sent(own.at[0, pl.ds(0, 448)], line_send.at[r])
        sent(own.at[1, pl.ds(0, 384)], y_send.at[r])
        sent(own.at[1, pl.ds(0, 448)], slice_send.at[r])
    sent(own.at[1, pl.ds(0, 128)], x_send.at[0])
    for tree in range(3):
        for way in range(3):
            if ONWARD[tree][way]:
                @pl.when(one_of(node, ONWARD[tree][way]))
                def _():
                    sent(rec.at[0, pl.ds(0, COUNT[tree] * CHUNK)], tree_send.at[tree, way])
    for u in range(2):
        swap(u).wait_send()
    for dl, dc in ((1, 0), (1, 1), (0, 1)):
        mix(dl, dc).wait_send()
    for g in range(4):
        l_mate(g).wait_send()
        l_twin(g).wait_send()
    for g in range(6):
        r_mate(g, SIZES[g]).wait_send()
        r_twin(g, SIZES[g]).wait_send()
        for part in range(PARTS[g]):
            stays, here, away = home(jnp.int32(g) if g < FAR else g, part)

            @pl.when(jnp.logical_not(stays))
            def _():
                away().wait_send()
    for half in range(2):
        l_out(half).wait()


def on_device(gradient, left_old, right_old):
    factor = jax.ShapeDtypeStruct((ROW, SUB), F32)
    anywhere = pl.BlockSpec(memory_space=pl.ANY)
    dma = pltpu.SemaphoreType.DMA
    gram_left, gram_right = pl.pallas_call(
        kernel,
        out_shape=(factor, factor),
        in_specs=[anywhere],
        out_specs=(anywhere, anywhere),
        scratch_shapes=[
            pltpu.VMEM((ROW, SUB), BF16), pltpu.VMEM((SUB, ROW), BF16),
            pltpu.VMEM((2, ROW, DEPTH), BF16), pltpu.VMEM((2, ROW, DEPTH), BF16),
            pltpu.VMEM((4, 2, 2, 64, ROW), F32), pltpu.VMEM((4, 2, 64, ROW), F32), pltpu.VMEM((4, 64, ROW), F32),
            pltpu.VMEM((4, 64, ROW), F32), pltpu.VMEM((SUB, ROW), F32),
            pltpu.VMEM((6, 2, 2, SUB, SUB), F32), pltpu.VMEM((6, 2, SUB, SUB), F32), pltpu.VMEM((6, SUB, SUB), F32),
            pltpu.VMEM((6, SUB, SUB), F32), pltpu.VMEM((6, SUB, SUB), F32), pltpu.VMEM((ROW, SUB), F32),
            dma((1,)), dma((2,)), dma((4,)), dma((4,)), dma((4,)), dma((2,)), dma((2, 14)), dma((1,)), dma((4,)), dma((2,)),
            dma((2, 12)), dma((2,)), dma((2, 14)), dma((3, 3)), dma((3, 22)), dma((1,)),
            dma((4,)), dma((4,)), dma((4,)), dma((4,)), dma((6,)), dma((6,)), dma((6,)), dma((6,)),
            dma((6, 2)), dma((RING,)), dma((2,)),
        ],
        compiler_params=pltpu.CompilerParams(collective_id=0, has_side_effects=True, vmem_limit_bytes=56 << 20),
        cost_estimate=pl.CostEstimate(flops=4 * ROW * SUB * 8192, bytes_accessed=5 << 20, transcendentals=0),
        name="gram_factors",
    )(gradient)
    return 0.95 * left_old + 0.05 * gram_left, 0.95 * right_old + 0.05 * gram_right


def solution(mesh):
    placed = (P("row", "col"), P("row", "col"), P("row", "col"))
    return jax.shard_map(
        on_device,
        mesh=mesh,
        in_specs=placed,
        out_specs=(P("row", "col"), P("row", "col")),
        check_vma=False,
    )
```
